256 devices in a mesh: occ: 16 (over z, y_lo), aux: 16 (over x, y_hi, core).
Axes of the slice: x: 4, y: 4 (y_hi: 2, y_lo: 2; y = y_hi * 2 + y_lo), z: 8, core: 2. Of those that a mesh axis runs over, the one named last changes fastest.
Arguments:
- factors: bfloat16 [16, 2048, 6144], P('occ', None, 'aux'), may hold values from -2.5 to 2.5
- eps_occ: float32 [32], replicated, may hold values from -2.5 to -0.3
- eps_vir: float32 [2048], replicated, may hold values from 0.2 to 3
- window_start: int32 [1], replicated, may hold values from 0 to 16
- assignment: int32 [16], replicated, may hold values from 0 to 15, each once
Outputs:
- gamma: float32 [16, 2048, 6144], P('occ', None, 'aux')
The draws below stay inside these ranges and needn't reach their ends.
Inputs may be any that keep to these rules, and one draw needn't show every extreme that they name: `assignment`: each number once.
All inputs are finite; a program needn't handle non-finite values.
Results may differ from the reference program's by a relative error of at most 0.0023.
Values may be sent and summed in bfloat16 or wider, within the bound.
A program may use at most 64 MiB of HBM per device.

```python
import math
import jax
import jax.numpy as jnp
from jax import lax

V = 2048
NAUX = 6144
NOCC = 16
OCC_ALL = 32


def draw_factors(key, part):
    key = jax.random.fold_in(key, 11)
    scale = (4.0 / math.sqrt(V * NAUX)) ** (1.0 / 3.0)
    key_main = jax.random.fold_in(key, 0)
    values = jax.random.normal(key_main, (NOCC, V, NAUX), jnp.float32)
    values = jnp.clip(values * scale, -4.0 * scale, 4.0 * scale)
    return values.astype(jnp.bfloat16)


def setup_inputs(seed: int = 0) -> dict:
    arg_keys = jax.random.split(jax.random.key(seed), 6)
    return {
        "factors": draw_factors(jax.random.fold_in(arg_keys[5], 71), 0),
        "eps_occ": jnp.clip(jax.random.uniform(arg_keys[1], (OCC_ALL,), jnp.float32, -2.5, -0.3), -2.5, -0.3),
        "eps_vir": jnp.clip(jax.random.uniform(arg_keys[2], (V,), jnp.float32, 0.2, 3.0), 0.2, 3.0),
        "window_start": jax.random.randint(arg_keys[3], (1,), 0, OCC_ALL - NOCC + 1).astype(jnp.int32),
        "assignment": jax.random.permutation(arg_keys[4], NOCC).astype(jnp.int32),
    }


def reference(factors, eps_occ, eps_vir, window_start, assignment):
    energy = eps_occ[window_start[0] + assignment]

    def pair(group):
        before = (group + NOCC - 1) % NOCC
        left = factors[group]
        right = factors[before]
        tile = lax.dot_general(right, left, (((1,), (1,)), ((), ())), preferred_element_type=jnp.float32)
        denom = eps_vir[:, None] + eps_vir[None, :] - energy[group] - energy[before]
        amplitude = (tile / denom).astype(jnp.bfloat16)
        own_part = lax.dot_general(amplitude, right, (((0,), (0,)), ((), ())), preferred_element_type=jnp.float32)
        back_part = jnp.dot(amplitude, left, preferred_element_type=jnp.float32)
        return own_part, back_part

    own_all, back_all = lax.map(pair, jnp.arange(NOCC, dtype=jnp.int32))
    return own_all + jnp.roll(back_all, -1, axis=0)
```

```python
import functools

import jax
import jax.numpy as jnp
from jax import lax
from jax.experimental import pallas as pl
from jax.experimental.pallas import tpu as pltpu
from jax.sharding import PartitionSpec as P

MESH = pl.DeviceIdType.MESH
NX, NY, NC = 4, 2, 2
BLOCKS = NX * NY
Y_LO, Y_ALL = 2, 4
ROWS = 64
PART = 128
GROUP = 256
AHEAD = 2


def dot(a, b, dims):
    return lax.dot_general(a, b, (dims, ((), ())), preferred_element_type=jnp.float32)


def kernel(
    n_occ, rows, eps_occ, start, assignment, own, eps_vir, out,
    left, right, tile, far_out, far, near, tail_via, tail, amp_via, amp, acc, back, back_in, acc_in, eps_rows, right_last, amp_last,
    local_sem, left_sem, right_sem, far_sem, near_sem, tail_sem, tail_via_sem,
    amp_y_sem, amp_y_via_sem, amp_x_sem, amp_f_sem, back_sem, acc_sem, right_last_sem, amp_last_sem,
):
    v, k = own.shape
    half_v = v // NC
    width = v // BLOCKS
    n = half_v // rows
    half = rows // 2
    per_part, per_group = PART // rows, GROUP // rows
    parts, first_last = half_v // PART, half_v - GROUP

    o = lax.axis_index("occ")
    u = lax.axis_index("aux")
    x, y, core = u // (NY * NC), (u // NC) % NY, u % NC
    o_next, o_prev = lax.rem(o + 1, n_occ), lax.rem(o + n_occ - 1, n_occ)
    x_next, x_prev, x_far = lax.rem(x + 1, NX), lax.rem(x + NX - 1, NX), lax.rem(x + 2, NX)

    def at(o_, x_, y_, c_):
        return (o_, (x_ * NY + y_) * NC + c_)

    sibling = at(o, x, y, 1 - core)

    def across(step):
        place = lax.rem(y * Y_LO + lax.rem(o, Y_LO) + step + Y_ALL, Y_ALL)
        return at((o // Y_LO) * Y_LO + lax.rem(place, Y_LO), x, place // Y_LO, core), place // Y_LO

    hop, _ = across(1 - 2 * core)
    hop_back, from_y = across(2 * core - 1)
    x_dev = (at(o, x_next, y, core), at(o, x_prev, y, core))
    next_dev = (at(o_next, x, y, 0), at(o_next, x, y, 1))
    prev_dev = (at(o_prev, x, y, 0), at(o_prev, x, y, 1))
    mine, theirs = x * NY + y, x * NY + 1 - y

    def remote(src, dst, sem, device, there=None):
        return pltpu.make_async_remote_copy(
            src_ref=src, dst_ref=dst, send_sem=sem.at[0], recv_sem=(sem if there is None else there).at[1],
            device_id=device, device_id_type=MESH,
        )

    def rds(c, size=rows, offset=0):
        return pl.ds(pl.multiple_of(c * rows + offset, 16), size)

    cols = lambda c_: pl.ds(pl.multiple_of(c_ * k, 128), k)
    pair_of = lambda x_: pl.ds(x_ * NY, NY)

    def left_copy():
        return remote(own, left.at[:, cols(core)], left_sem, sibling)

    def prds(p):
        return pl.ds(pl.multiple_of(p * PART, 16), PART)

    def right_copy(p, d):
        src = own.at[pl.ds(pl.multiple_of(d * half_v + p * PART, 16), PART), :]
        return remote(
            src, right.at[prds(p), cols(core)], right_sem.at[p, d], next_dev[d], right_sem.at[p, core]
        )

    def right_arrival(p, s):
        src = own.at[pl.ds(0, PART), :]
        return remote(src, right.at[prds(p), cols(s)], right_sem.at[p, s], next_dev[s])

    def right_last_copy(p):
        r = pl.ds(pl.multiple_of(p * PART - first_last, 16), PART)
        i = p - first_last // PART
        return remote(right.at[prds(p), cols(1 - core)], right_last.at[r, :], right_last_sem.at[i], sibling)

    def far_copy(c, d):
        r = rds(c, half, d * half)
        return remote(far_out.at[:, r, :], far.at[:, r, :], far_sem.at[c, d], x_dev[d])

    def near_copy(c, d):
        src = tile.at[pair_of((x_next, x_prev)[d]), rds(c), :]
        return remote(src, near.at[d, :, rds(c), :], near_sem.at[c, d], x_dev[d])

    def tail_copy(c):
        return remote(tile.at[theirs, rds(c), :], tail_via.at[rds(c), :], tail_via_sem.at[c], hop)

    def tail_pass(c):
        return remote(tail_via.at[rds(c), :], tail.at[rds(c), :], tail_sem.at[c], hop)

    def amp_y_copy(c):
        return remote(amp.at[mine, rds(c), :], amp_via.at[rds(c), :], amp_y_via_sem.at[c], hop)

    def amp_y_pass(c, block):
        return remote(amp_via.at[rds(c), :], amp.at[block, rds(c), :], amp_y_sem.at[c], hop)

    def amp_x_copy(c, d, x_=x):
        block = amp.at[pair_of(x_), rds(c), :]
        return remote(block, block, amp_x_sem.at[c, d], x_dev[d])

    def amp_f_copy(c, d, x_):
        block = amp.at[pair_of(x_), rds(c, half, d * half), :]
        return remote(block, block, amp_f_sem.at[c, d], x_dev[d])

    def amp_last_copy(c):
        r = pl.ds(pl.multiple_of(c * rows - first_last, 16), rows)
        return remote(amp.at[:, rds(c), :], amp_last.at[:, r, :], amp_last_sem.at[c - (n - per_group)], sibling)

    def back_copy(p, d):
        dst = back_in.at[pl.ds(pl.multiple_of(core * half_v + p * PART, 16), PART), :]
        return remote(back.at[prds(p), cols(d)], dst, back_sem.at[p, d], prev_dev[d], back_sem.at[p, core])

    def back_arrival(p, s):
        dst = back_in.at[pl.ds(pl.multiple_of(s * half_v + p * PART, 16), PART), :]
        return remote(back.at[prds(p), cols(s)], dst, back_sem.at[p, s], prev_dev[s])

    def acc_copy(b):
        return remote(acc.at[b, :, cols(1 - core)], acc_in.at[b], acc_sem.at[b], sibling)

    barrier = pltpu.get_barrier_semaphore()
    others = (sibling, hop, hop_back) + x_dev + next_dev + prev_dev
    for device in others:
        pl.semaphore_signal(barrier, inc=1, device_id=device, device_id_type=MESH)
    local = pltpu.make_async_copy(own, left.at[:, cols(core)], local_sem)
    local.start()

    for i in range(half_v // min(128, half_v)):
        m = min(128, half_v)
        line = eps_vir[:, pl.ds(pl.multiple_of(core * half_v + i * m, m), m)]
        eps_rows[pl.ds(i * m, m), :] = jnp.broadcast_to(line, (m, m)).T
    for b in range(BLOCKS):
        acc[b] = jnp.zeros((width, NC * k), jnp.float32)
    slot = start[0]
    occ_sum = eps_occ[slot + assignment[o]] + eps_occ[slot + assignment[o_prev]]
    eps_cols = eps_vir[:, pl.ds(pl.multiple_of(mine * width, width), width)] - occ_sum

    pl.semaphore_wait(barrier, len(others))

    def send_right(p):
        for d in range(NC):
            right_copy(p, d).start()

    left_copy().start()
    for p in range(min(AHEAD, parts)):
        send_right(p)
    local.wait()
    left_copy().wait_recv()

    def tile_block(p, x_):
        block = left[pl.ds(pl.multiple_of(x_ * NY * width, NY * width), NY * width), :]
        return dot(right[prds(p), :], block, ((1,), (1,)))

    def stage_tile(c):
        p = c // per_part

        @pl.when(lax.rem(c, per_part) == 0)
        def _():
            @pl.when(p + AHEAD < parts)
            def _():
                send_right(p + AHEAD)

            for s in range(NC):
                right_arrival(p, s).wait_recv()

            @pl.when(p >= first_last // PART)
            def _():
                right_last_copy(p).start()

            values = tile_block(p, x_far).astype(jnp.bfloat16)
            for j in range(NY):
                far_out[j, prds(p), :] = values[:, j * width : (j + 1) * width]

        for d in range(2):
            far_copy(c, d).start()

        @pl.when(lax.rem(c, per_part) == 0)
        def _():
            for x_ in (x_next, x_prev, x):
                values = tile_block(p, x_)
                for j in range(NY):
                    tile[x_ * NY + j, prds(p), :] = values[:, j * width : (j + 1) * width]

    def stage_near(c):
        for d in range(2):
            far_copy(c, d).wait_recv()
            x_ = (x_next, x_prev)[d]
            r = rds(c, half, d * half)
            for j in range(NY):
                tile[x_ * NY + j, r, :] += far[j, r, :].astype(jnp.float32)
        for d in range(2):
            near_copy(c, d).start()

    def stage_sum(c):
        for d in range(2):
            near_copy(c, d).wait_recv()
        r = rds(c)
        tile[theirs, r, :] += near[0, 1 - y, r, :] + near[1, 1 - y, r, :]
        tail_copy(c).start()
        tile[mine, r, :] += near[0, y, r, :] + near[1, y, r, :]

    def stage_tail(c):
        tail_copy(c).wait_recv()
        tail_pass(c).start()

    def stage_amp(c):
        tail_pass(c).wait_recv()
        r = rds(c)
        total = tile[mine, r, :] + tail[r, :]
        denominator = eps_rows[r, 0:1] + eps_cols
        amp[mine, r, :] = (total / denominator).astype(jnp.bfloat16)
        amp_y_copy(c).start()

    def stage_amp_pass(c):
        amp_y_copy(c).wait_recv()
        amp_y_pass(c, x * NY + from_y).start()

    def stage_spread(c):
        amp_y_pass(c, theirs).wait_recv()
        for d in range(2):
            amp_x_copy(c, d).start()

    def stage_forward(c):
        for d in range(2):
            amp_x_copy(c, d, (x_prev, x_next)[d]).wait_recv()
            amp_f_copy(c, d, (x_prev, x_next)[d]).start()

    def own_block(first, b):
        r = pl.ds(pl.multiple_of(first * rows, 16), GROUP)
        acc[b] += dot(amp[b, r, :], right[r, :], ((0,), (0,)))

    def stage_gamma(c):
        for d in range(2):
            amp_f_copy(c, d, x_far).wait_recv()

        @pl.when(c >= n - per_group)
        def _():
            amp_last_copy(c).start()

        @pl.when(lax.rem(c + 1, per_part) == 0)
        def _():
            p = c // per_part
            r = prds(p)
            total = dot(amp[0, r, :], left[pl.ds(0, width), :], ((1,), (0,)))
            for b in range(1, BLOCKS):
                total += dot(amp[b, r, :], left[pl.ds(b * width, width), :], ((1,), (0,)))
            back[r, :] = total.astype(jnp.bfloat16)
            for d in range(NC):
                back_copy(p, d).start()

        @pl.when((lax.rem(c + 1, per_group) == 0) & (c + 1 < n))
        def _():
            for b in range(BLOCKS):
                own_block(c + 1 - per_group, b)

            @pl.when(c + 1 == n - per_group)
            def _():
                for b in range(BLOCKS):
                    acc_copy(b).start()

    stages = (
        stage_tile, stage_gamma, stage_forward, stage_spread, stage_amp_pass, stage_amp, stage_tail, stage_sum, stage_near,
    )
    offsets = (0, 16, 14, 12, 10, 8, 6, 4, 2)

    def tick(t, carry):
        for stage, offset in zip(stages, offsets):
            c = t - offset

            @pl.when((c >= 0) & (c < n))
            def _():
                stage(c)

        return carry

    lax.fori_loop(0, n + max(offsets), tick, 0)

    for p in range(first_last // PART, parts):
        right_last_copy(p).wait_recv()
    for c in range(n - per_group, n):
        amp_last_copy(c).wait_recv()
    for b in range(BLOCKS):
        acc_copy(b).wait_recv()

    last = pl.ds(first_last, GROUP)
    for b in range(BLOCKS):
        total = acc[b, :, cols(core)] + acc_in[b]
        total += dot(amp[b, last, :], right[last, cols(core)], ((0,), (0,)))
        total += dot(amp_last[b], right_last[...], ((0,), (0,)))
        out[pl.ds(b * width, width), :] = total

    def arrived(p, carry):
        for s in range(NC):
            back_arrival(p, s).wait_recv()
        return carry

    lax.fori_loop(0, parts, arrived, 0)
    for b in range(BLOCKS):
        r = pl.ds(b * width, width)
        out[r, :] += back_in[r, :].astype(jnp.float32)

    left_copy().wait_send()
    for b in range(BLOCKS):
        acc_copy(b).wait_send()
    for p in range(first_last // PART, parts):
        right_last_copy(p).wait_send()
    for c in range(n - per_group, n):
        amp_last_copy(c).wait_send()

    def part_sent(p, carry):
        for d in range(NC):
            right_copy(p, d).wait_send()
            back_copy(p, d).wait_send()
        return carry

    lax.fori_loop(0, parts, part_sent, 0)

    def sent(c, carry):
        for d in range(2):
            far_copy(c, d).wait_send()
            near_copy(c, d).wait_send()
            amp_x_copy(c, d).wait_send()
            amp_f_copy(c, d, (x_prev, x_next)[d]).wait_send()
        tail_copy(c).wait_send()
        tail_pass(c).wait_send()
        amp_y_copy(c).wait_send()
        amp_y_pass(c, x * NY + from_y).wait_send()
        return carry

    lax.fori_loop(0, n, sent, 0)


def per_device(n_occ, rows, factors, eps_occ, eps_vir, window_start, assignment):
    own = factors[0]
    v, k = own.shape
    half_v, width = v // NC, v // BLOCKS
    n = half_v // rows
    f32, bf16 = jnp.float32, jnp.bfloat16
    dma = pltpu.SemaphoreType.DMA
    smem = pl.BlockSpec(memory_space=pltpu.SMEM)
    out = pl.pallas_call(
        functools.partial(kernel, n_occ, rows),
        out_shape=jax.ShapeDtypeStruct((v, k), f32),
        in_specs=[smem, smem, smem, pl.BlockSpec(memory_space=pl.ANY), pl.BlockSpec(memory_space=pltpu.VMEM)],
        out_specs=pl.BlockSpec(memory_space=pltpu.VMEM),
        scratch_shapes=[
            pltpu.VMEM((v, NC * k), bf16),
            pltpu.VMEM((half_v, NC * k), bf16),
            pltpu.VMEM((BLOCKS, half_v, width), f32),
            pltpu.VMEM((NY, half_v, width), bf16),
            pltpu.VMEM((NY, half_v, width), bf16),
            pltpu.VMEM((2, NY, half_v, width), f32),
            pltpu.VMEM((half_v, width), f32),
            pltpu.VMEM((half_v, width), f32),
            pltpu.VMEM((half_v, width), bf16),
            pltpu.VMEM((BLOCKS, half_v, width), bf16),
            pltpu.VMEM((BLOCKS, width, NC * k), f32),
            pltpu.VMEM((half_v, NC * k), bf16),
            pltpu.VMEM((v, k), bf16),
            pltpu.VMEM((BLOCKS, width, k), f32),
            pltpu.VMEM((half_v, min(128, half_v)), f32),
            pltpu.VMEM((GROUP, k), bf16),
            pltpu.VMEM((BLOCKS, GROUP, width), bf16),
            dma(()),
            dma((2,)),
            dma((half_v // PART, 2, 2)),
            dma((n, 2, 2)),
            dma((n, 2, 2)),
            dma((n, 2)),
            dma((n, 2)),
            dma((n, 2)),
            dma((n, 2)),
            dma((n, 2, 2)),
            dma((n, 2, 2)),
            dma((half_v // PART, 2, 2)),
            dma((BLOCKS, 2)),
            dma((GROUP // PART, 2)),
            dma((GROUP // rows, 2)),
        ],
        compiler_params=pltpu.CompilerParams(
            collective_id=0, has_side_effects=True, vmem_limit_bytes=60 * 2**20
        ),
        cost_estimate=pl.CostEstimate(
            flops=3 * 2 * v * v * k, bytes_accessed=6 * v * k, transcendentals=0
        ),
    )(eps_occ, window_start, assignment, own, eps_vir[None, :])
    return out[None]


def solution(mesh):
    in_specs = (P("occ", None, "aux"), P(), P(), P(), P())
    out_specs = P("occ", None, "aux")
    return jax.shard_map(
        functools.partial(per_device, mesh.shape["occ"], ROWS),
        mesh=mesh, in_specs=in_specs, out_specs=out_specs, check_vma=False,
    )
```

```python
import functools

import jax
import jax.numpy as jnp
from jax import lax
from jax.experimental import pallas as pl
from jax.experimental.pallas import tpu as pltpu
from jax.sharding import PartitionSpec as P

MESH = pl.DeviceIdType.MESH
NX, NY, NC = 4, 2, 2
BLOCKS = NX * NY
ROWS = 64
PART = 64
GROUP = 256
AHEAD = 4


def dot(a, b, dims):
    return lax.dot_general(a, b, (dims, ((), ())), preferred_element_type=jnp.float32)


def fixed(values):
    top = functools.reduce(jnp.maximum, [jnp.abs(v) for v in values])
    top = jnp.max(jnp.max(top, axis=0, keepdims=True), axis=1, keepdims=True)
    top = jnp.maximum(top, 1e-30)
    return [jnp.round(v * (32767.0 / top)).astype(jnp.int16) for v in values], top * (1 / 32767.0)


def kernel(
    n_occ, rows, eps_occ, start, assignment, own, eps_vir, out,
    left, right, tile, far_out, far, near_out, near, near_unit_out, near_unit,
    tail_out, tail, tail_unit_out, tail_unit, amp, acc, back, back_in, acc_in, eps_rows, right_last, amp_last,
    local_sem, left_sem, right_sem, far_sem, near_sem, near_unit_sem,
    tail_sem, tail_unit_sem,
    amp_y_sem, amp_x_sem, amp_f_sem, back_sem, acc_sem, right_last_sem, amp_last_sem,
):
    v, k = own.shape
    half_v = v // NC
    width = v // BLOCKS
    n = half_v // rows
    half = rows // 2
    per_part, per_group = PART // rows, GROUP // rows
    parts, first_last = half_v // PART, half_v - GROUP

    o = lax.axis_index("occ")
    u = lax.axis_index("aux")
    x, y, core = u // (NY * NC), (u // NC) % NY, u % NC
    o_next, o_prev = lax.rem(o + 1, n_occ), lax.rem(o + n_occ - 1, n_occ)
    x_next, x_prev, x_far = lax.rem(x + 1, NX), lax.rem(x + NX - 1, NX), lax.rem(x + 2, NX)

    def at(o_, x_, y_, c_):
        return (o_, (x_ * NY + y_) * NC + c_)

    sibling = at(o, x, y, 1 - core)
    partner = at(o, x, 1 - y, core)
    x_dev = (at(o, x_next, y, core), at(o, x_prev, y, core))
    next_dev = (at(o_next, x, y, 0), at(o_next, x, y, 1))
    prev_dev = (at(o_prev, x, y, 0), at(o_prev, x, y, 1))
    mine, theirs = x * NY + y, x * NY + 1 - y

    def remote(src, dst, sem, device, there=None):
        return pltpu.make_async_remote_copy(
            src_ref=src, dst_ref=dst, send_sem=sem.at[0], recv_sem=(sem if there is None else there).at[1],
            device_id=device, device_id_type=MESH,
        )

    def rds(c, size=rows, offset=0):
        return pl.ds(pl.multiple_of(c * rows + offset, 16), size)

    cols = lambda c_: pl.ds(pl.multiple_of(c_ * k, 128), k)
    pair_of = lambda x_: pl.ds(x_ * NY, NY)

    def left_copy():
        return remote(own, left.at[:, cols(core)], left_sem, sibling)

    def prds(p):
        return pl.ds(pl.multiple_of(p * PART, 16), PART)

    def right_copy(p, d):
        src = own.at[pl.ds(pl.multiple_of(d * half_v + p * PART, 16), PART), :]
        return remote(
            src, right.at[prds(p), cols(core)], right_sem.at[p, d], next_dev[d], right_sem.at[p, core]
        )

    def right_arrival(p, s):
        src = own.at[pl.ds(0, PART), :]
        return remote(src, right.at[prds(p), cols(s)], right_sem.at[p, s], next_dev[s])

    def right_last_copy(p):
        r = pl.ds(pl.multiple_of(p * PART - first_last, 16), PART)
        i = p - first_last // PART
        return remote(right.at[prds(p), cols(1 - core)], right_last.at[r, :], right_last_sem.at[i], sibling)

    def far_copy(c, d):
        r = rds(c, half, d * half)
        return remote(far_out.at[:, r, :], far.at[:, r, :], far_sem.at[c, d], x_dev[d])

    def near_copy(c, d):
        return remote(near_out.at[d, :, rds(c), :], near.at[d, :, rds(c), :], near_sem.at[c, d], x_dev[d])

    def near_unit_copy(c, d):
        return remote(near_unit_out.at[c, d], near_unit.at[c, d], near_unit_sem.at[c, d], x_dev[d])

    def tail_copy(c):
        return remote(tail_out.at[rds(c), :], tail.at[rds(c), :], tail_sem.at[c], partner)

    def tail_unit_copy(c):
        return remote(tail_unit_out.at[c], tail_unit.at[c], tail_unit_sem.at[c], partner)

    def amp_y_copy(c, block=mine):
        block = amp.at[block, rds(c), :]
        return remote(block, block, amp_y_sem.at[c], partner)

    def amp_x_copy(c, d, x_=x):
        block = amp.at[pair_of(x_), rds(c), :]
        return remote(block, block, amp_x_sem.at[c, d], x_dev[d])

    def amp_f_copy(c, d, x_):
        block = amp.at[pair_of(x_), rds(c, half, d * half), :]
        return remote(block, block, amp_f_sem.at[c, d], x_dev[d])

    def amp_last_copy(c):
        r = pl.ds(pl.multiple_of(c * rows - first_last, 16), rows)
        return remote(amp.at[:, rds(c), :], amp_last.at[:, r, :], amp_last_sem.at[c - (n - per_group)], sibling)

    def back_copy(p, d):
        dst = back_in.at[pl.ds(pl.multiple_of(core * half_v + p * PART, 16), PART), :]
        return remote(back.at[prds(p), cols(d)], dst, back_sem.at[p, d], prev_dev[d], back_sem.at[p, core])

    def back_arrival(p, s):
        dst = back_in.at[pl.ds(pl.multiple_of(s * half_v + p * PART, 16), PART), :]
        return remote(back.at[prds(p), cols(s)], dst, back_sem.at[p, s], prev_dev[s])

    def acc_copy(b):
        return remote(acc.at[b, :, cols(1 - core)], acc_in.at[b], acc_sem.at[b], sibling)

    barrier = pltpu.get_barrier_semaphore()
    others = (sibling, partner) + x_dev + next_dev + prev_dev
    for device in others:
        pl.semaphore_signal(barrier, inc=1, device_id=device, device_id_type=MESH)
    local = pltpu.make_async_copy(own, left.at[:, cols(core)], local_sem)
    local.start()

    for i in range(half_v // min(128, half_v)):
        m = min(128, half_v)
        line = eps_vir[:, pl.ds(pl.multiple_of(core * half_v + i * m, m), m)]
        eps_rows[pl.ds(i * m, m), :] = jnp.broadcast_to(line, (m, m)).T
    for b in range(BLOCKS):
        acc[b] = jnp.zeros((width, NC * k), jnp.float32)
    slot = start[0]
    occ_sum = eps_occ[slot + assignment[o]] + eps_occ[slot + assignment[o_prev]]
    eps_cols = eps_vir[:, pl.ds(pl.multiple_of(mine * width, width), width)] - occ_sum

    pl.semaphore_wait(barrier, len(others))

    def send_right(p):
        for d in range(NC):
            right_copy(p, d).start()

    left_copy().start()
    for p in range(min(AHEAD, parts)):
        send_right(p)
    local.wait()
    left_copy().wait_recv()

    def tile_block(p, x_):
        block = left[pl.ds(pl.multiple_of(x_ * NY * width, NY * width), NY * width), :]
        return dot(right[prds(p), :], block, ((1,), (1,)))

    def stage_tile(c):
        p = c // per_part

        @pl.when(lax.rem(c, per_part) == 0)
        def _():
            @pl.when(p + AHEAD < parts)
            def _():
                send_right(p + AHEAD)

            for s in range(NC):
                right_arrival(p, s).wait_recv()

            @pl.when(p >= first_last // PART)
            def _():
                right_last_copy(p).start()

            values = tile_block(p, x_far).astype(jnp.bfloat16)
            for j in range(NY):
                far_out[j, prds(p), :] = values[:, j * width : (j + 1) * width]

        for d in range(2):
            far_copy(c, d).start()

        @pl.when(lax.rem(c, per_part) == 0)
        def _():
            for x_ in (x_next, x_prev, x):
                values = tile_block(p, x_)
                for j in range(NY):
                    tile[x_ * NY + j, prds(p), :] = values[:, j * width : (j + 1) * width]

    def stage_near(c):
        for d in range(2):
            far_copy(c, d).wait_recv()
            x_ = (x_next, x_prev)[d]
            r = rds(c, half, d * half)
            for j in range(NY):
                tile[x_ * NY + j, r, :] += far[j, r, :].astype(jnp.float32)
            codes, unit = fixed([tile[x_ * NY + j, rds(c), :] for j in range(NY)])
            for j in range(NY):
                near_out[d, j, rds(c), :] = codes[j]
            near_unit_out[c, d] = jnp.broadcast_to(unit, near_unit_out.shape[2:])
            near_unit_copy(c, d).start()
            near_copy(c, d).start()

    def near_sum(c, y_):
        r = rds(c)
        total = tile[x * NY + y_, r, :]
        for d in range(2):
            total += near[d, y_, r, :].astype(jnp.float32) * near_unit[c, d][0:1, 0:1]
        return total

    def stage_sum(c):
        for d in range(2):
            near_unit_copy(c, d).wait_recv()
            near_copy(c, d).wait_recv()
        (codes,), unit = fixed([near_sum(c, 1 - y)])
        tail_out[rds(c), :] = codes
        tail_unit_out[c] = jnp.broadcast_to(unit, tail_unit_out.shape[1:])
        tail_unit_copy(c).start()
        tail_copy(c).start()
        tile[mine, rds(c), :] = near_sum(c, y)

    def stage_amp(c):
        tail_unit_copy(c).wait_recv()
        tail_copy(c).wait_recv()
        r = rds(c)
        total = tile[mine, r, :] + tail[r, :].astype(jnp.float32) * tail_unit[c][0:1, 0:1]
        denominator = eps_rows[r, 0:1] + eps_cols
        amp[mine, r, :] = (total / denominator).astype(jnp.bfloat16)
        amp_y_copy(c).start()

    def stage_spread(c):
        amp_y_copy(c, theirs).wait_recv()
        for d in range(2):
            amp_x_copy(c, d).start()

    def stage_forward(c):
        for d in range(2):
            amp_x_copy(c, d, (x_prev, x_next)[d]).wait_recv()
            amp_f_copy(c, d, (x_prev, x_next)[d]).start()

    def own_block(first, b):
        r = pl.ds(pl.multiple_of(first * rows, 16), GROUP)
        acc[b] += dot(amp[b, r, :], right[r, :], ((0,), (0,)))

    def stage_gamma(c):
        for d in range(2):
            amp_f_copy(c, d, x_far).wait_recv()

        @pl.when(c >= n - per_group)
        def _():
            amp_last_copy(c).start()

        @pl.when(lax.rem(c + 1, per_part) == 0)
        def _():
            p = c // per_part
            r = prds(p)
            total = dot(amp[0, r, :], left[pl.ds(0, width), :], ((1,), (0,)))
            for b in range(1, BLOCKS):
                total += dot(amp[b, r, :], left[pl.ds(b * width, width), :], ((1,), (0,)))
            back[r, :] = total.astype(jnp.bfloat16)
            for d in range(NC):
                back_copy(p, d).start()

        @pl.when((lax.rem(c + 1, per_group) == 0) & (c + 1 < n))
        def _():
            for b in range(BLOCKS):
                own_block(c + 1 - per_group, b)

            @pl.when(c + 1 == n - per_group)
            def _():
                for b in range(BLOCKS):
                    acc_copy(b).start()

    stages = (stage_tile, stage_gamma, stage_forward, stage_spread, stage_amp, stage_sum, stage_near)
    offsets = (0, 14, 11, 8, 6, 4, 2)

    def tick(t, carry):
        for stage, offset in zip(stages, offsets):
            c = t - offset

            @pl.when((c >= 0) & (c < n))
            def _():
                stage(c)

        return carry

    lax.fori_loop(0, n + max(offsets), tick, 0)

    for p in range(first_last // PART, parts):
        right_last_copy(p).wait_recv()
    for c in range(n - per_group, n):
        amp_last_copy(c).wait_recv()
    for b in range(BLOCKS):
        acc_copy(b).wait_recv()

    last = pl.ds(first_last, GROUP)
    for b in range(BLOCKS):
        total = acc[b, :, cols(core)] + acc_in[b]
        total += dot(amp[b, last, :], right[last, cols(core)], ((0,), (0,)))
        total += dot(amp_last[b], right_last[...], ((0,), (0,)))
        out[pl.ds(b * width, width), :] = total

    def arrived(p, carry):
        for s in range(NC):
            back_arrival(p, s).wait_recv()
        return carry

    lax.fori_loop(0, parts, arrived, 0)
    for b in range(BLOCKS):
        r = pl.ds(b * width, width)
        out[r, :] += back_in[r, :].astype(jnp.float32)

    left_copy().wait_send()
    for b in range(BLOCKS):
        acc_copy(b).wait_send()
    for p in range(first_last // PART, parts):
        right_last_copy(p).wait_send()
    for c in range(n - per_group, n):
        amp_last_copy(c).wait_send()

    def part_sent(p, carry):
        for d in range(NC):
            right_copy(p, d).wait_send()
            back_copy(p, d).wait_send()
        return carry

    lax.fori_loop(0, parts, part_sent, 0)

    def sent(c, carry):
        for d in range(2):
            far_copy(c, d).wait_send()
            near_copy(c, d).wait_send()
            near_unit_copy(c, d).wait_send()
            amp_x_copy(c, d).wait_send()
            amp_f_copy(c, d, (x_prev, x_next)[d]).wait_send()
        tail_copy(c).wait_send()
        tail_unit_copy(c).wait_send()
        amp_y_copy(c).wait_send()
        return carry

    lax.fori_loop(0, n, sent, 0)


def per_device(n_occ, rows, factors, eps_occ, eps_vir, window_start, assignment):
    own = factors[0]
    v, k = own.shape
    half_v, width = v // NC, v // BLOCKS
    n = half_v // rows
    f32, bf16 = jnp.float32, jnp.bfloat16
    dma = pltpu.SemaphoreType.DMA
    smem = pl.BlockSpec(memory_space=pltpu.SMEM)
    out = pl.pallas_call(
        functools.partial(kernel, n_occ, rows),
        out_shape=jax.ShapeDtypeStruct((v, k), f32),
        in_specs=[smem, smem, smem, pl.BlockSpec(memory_space=pl.ANY), pl.BlockSpec(memory_space=pltpu.VMEM)],
        out_specs=pl.BlockSpec(memory_space=pltpu.VMEM),
        scratch_shapes=[
            pltpu.VMEM((v, NC * k), bf16),
            pltpu.VMEM((half_v, NC * k), bf16),
            pltpu.VMEM((BLOCKS, half_v, width), f32),
            pltpu.VMEM((NY, half_v, width), bf16),
            pltpu.VMEM((NY, half_v, width), bf16),
            pltpu.VMEM((2, NY, half_v, width), jnp.int16),
            pltpu.VMEM((2, NY, half_v, width), jnp.int16),
            pltpu.VMEM((n, 2, 8, 128), f32),
            pltpu.VMEM((n, 2, 8, 128), f32),
            pltpu.VMEM((half_v, width), jnp.int16),
            pltpu.VMEM((half_v, width), jnp.int16),
            pltpu.VMEM((n, 8, 128), f32),
            pltpu.VMEM((n, 8, 128), f32),
            pltpu.VMEM((BLOCKS, half_v, width), bf16),
            pltpu.VMEM((BLOCKS, width, NC * k), f32),
            pltpu.VMEM((half_v, NC * k), bf16),
            pltpu.VMEM((v, k), bf16),
            pltpu.VMEM((BLOCKS, width, k), f32),
            pltpu.VMEM((half_v, min(128, half_v)), f32),
            pltpu.VMEM((GROUP, k), bf16),
            pltpu.VMEM((BLOCKS, GROUP, width), bf16),
            dma(()),
            dma((2,)),
            dma((half_v // PART, 2, 2)),
            dma((n, 2, 2)),
            dma((n, 2, 2)),
            dma((n, 2, 2)),
            dma((n, 2)),
            dma((n, 2)),
            dma((n, 2)),
            dma((n, 2, 2)),
            dma((n, 2, 2)),
            dma((half_v // PART, 2, 2)),
            dma((BLOCKS, 2)),
            dma((GROUP // PART, 2)),
            dma((GROUP // rows, 2)),
        ],
        compiler_params=pltpu.CompilerParams(
            collective_id=0, has_side_effects=True, vmem_limit_bytes=60 * 2**20
        ),
        cost_estimate=pl.CostEstimate(
            flops=3 * 2 * v * v * k, bytes_accessed=6 * v * k, transcendentals=0
        ),
    )(eps_occ, window_start, assignment, own, eps_vir[None, :])
    return out[None]


def solution(mesh):
    in_specs = (P("occ", None, "aux"), P(), P(), P(), P())
    out_specs = P("occ", None, "aux")
    return jax.shard_map(
        functools.partial(per_device, mesh.shape["occ"], ROWS),
        mesh=mesh, in_specs=in_specs, out_specs=out_specs, check_vma=False,
    )
```

```python
import functools

import jax
import jax.numpy as jnp
from jax import lax
from jax.experimental import pallas as pl
from jax.experimental.pallas import tpu as pltpu
from jax.sharding import PartitionSpec as P

MESH = pl.DeviceIdType.MESH
NX, NY, NC = 4, 2, 2
BLOCKS = NX * NY
ROWS = 64
PART = 64
GROUP = 256
AHEAD = 4


def dot(a, b, dims):
    return lax.dot_general(a, b, (dims, ((), ())), preferred_element_type=jnp.float32)


def fixed(values):
    top = functools.reduce(jnp.maximum, [jnp.abs(v) for v in values])
    top = jnp.max(jnp.max(top, axis=0, keepdims=True), axis=1, keepdims=True)
    top = jnp.maximum(top, 1e-30)
    return [jnp.round(v * (32767.0 / top)).astype(jnp.int16) for v in values], top * (1 / 32767.0)


def kernel(
    n_occ, rows, eps_occ, start, assignment, own, eps_vir, out,
    left, right, tile, far_out, far, near_out, near, near_unit_out, near_unit,
    tail_out, tail, tail_unit_out, tail_unit, amp, acc, back, back_in, acc_in, eps_rows, right_last, amp_last,
    local_sem, left_sem, right_sem, far_sem, near_sem, near_unit_sem,
    tail_sem, tail_unit_sem,
    amp_x_sem, amp_f_sem, back_sem, acc_sem, right_last_sem, amp_last_sem,
):
    v, k = own.shape
    half_v = v // NC
    width = v // BLOCKS
    n = half_v // rows
    half = rows // 2
    per_part, per_group = PART // rows, GROUP // rows
    parts, first_last = half_v // PART, half_v - GROUP

    o = lax.axis_index("occ")
    u = lax.axis_index("aux")
    x, y, core = u // (NY * NC), (u // NC) % NY, u % NC
    o_next, o_prev = lax.rem(o + 1, n_occ), lax.rem(o + n_occ - 1, n_occ)
    x_next, x_prev, x_far = lax.rem(x + 1, NX), lax.rem(x + NX - 1, NX), lax.rem(x + 2, NX)

    def at(o_, x_, y_, c_):
        return (o_, (x_ * NY + y_) * NC + c_)

    sibling = at(o, x, y, 1 - core)
    partner = at(o, x, 1 - y, core)
    x_dev = (at(o, x_next, y, core), at(o, x_prev, y, core))
    next_dev = (at(o_next, x, y, 0), at(o_next, x, y, 1))
    prev_dev = (at(o_prev, x, y, 0), at(o_prev, x, y, 1))

    def remote(src, dst, sem, device, there=None):
        return pltpu.make_async_remote_copy(
            src_ref=src, dst_ref=dst, send_sem=sem.at[0], recv_sem=(sem if there is None else there).at[1],
            device_id=device, device_id_type=MESH,
        )

    def rds(c, size=rows, offset=0):
        return pl.ds(pl.multiple_of(c * rows + offset, 16), size)

    cols = lambda c_: pl.ds(pl.multiple_of(c_ * k, 128), k)
    pair_of = lambda x_: pl.ds(x_ * NY, NY)

    def left_copy():
        return remote(own, left.at[:, cols(core)], left_sem, sibling)

    def prds(p):
        return pl.ds(pl.multiple_of(p * PART, 16), PART)

    def right_copy(p, d):
        src = own.at[pl.ds(pl.multiple_of(d * half_v + p * PART, 16), PART), :]
        return remote(
            src, right.at[prds(p), cols(core)], right_sem.at[p, d], next_dev[d], right_sem.at[p, core]
        )

    def right_arrival(p, s):
        src = own.at[pl.ds(0, PART), :]
        return remote(src, right.at[prds(p), cols(s)], right_sem.at[p, s], next_dev[s])

    def right_last_copy(p):
        r = pl.ds(pl.multiple_of(p * PART - first_last, 16), PART)
        i = p - first_last // PART
        return remote(right.at[prds(p), cols(1 - core)], right_last.at[r, :], right_last_sem.at[i], sibling)

    def far_copy(c, d):
        r = rds(c, half, d * half)
        return remote(far_out.at[:, r, :], far.at[:, r, :], far_sem.at[c, d], x_dev[d])

    def near_copy(c, d):
        return remote(near_out.at[d, :, rds(c), :], near.at[d, :, rds(c), :], near_sem.at[c, d], x_dev[d])

    def near_unit_copy(c, d):
        return remote(near_unit_out.at[c, d], near_unit.at[c, d], near_unit_sem.at[c, d], x_dev[d])

    def tail_copy(c):
        return remote(tail_out.at[:, rds(c), :], tail.at[:, rds(c), :], tail_sem.at[c], partner)

    def tail_unit_copy(c):
        return remote(tail_unit_out.at[c], tail_unit.at[c], tail_unit_sem.at[c], partner)

    def amp_x_copy(c, d, x_=x):
        block = amp.at[pair_of(x_), rds(c), :]
        return remote(block, block, amp_x_sem.at[c, d], x_dev[d])

    def amp_f_copy(c, d, x_):
        block = amp.at[pair_of(x_), rds(c, half, d * half), :]
        return remote(block, block, amp_f_sem.at[c, d], x_dev[d])

    def amp_last_copy(c):
        r = pl.ds(pl.multiple_of(c * rows - first_last, 16), rows)
        return remote(amp.at[:, rds(c), :], amp_last.at[:, r, :], amp_last_sem.at[c - (n - per_group)], sibling)

    def back_copy(p, d):
        dst = back_in.at[pl.ds(pl.multiple_of(core * half_v + p * PART, 16), PART), :]
        return remote(back.at[prds(p), cols(d)], dst, back_sem.at[p, d], prev_dev[d], back_sem.at[p, core])

    def back_arrival(p, s):
        dst = back_in.at[pl.ds(pl.multiple_of(s * half_v + p * PART, 16), PART), :]
        return remote(back.at[prds(p), cols(s)], dst, back_sem.at[p, s], prev_dev[s])

    def acc_copy(b):
        return remote(acc.at[b, :, cols(1 - core)], acc_in.at[b], acc_sem.at[b], sibling)

    barrier = pltpu.get_barrier_semaphore()
    others = (sibling, partner) + x_dev + next_dev + prev_dev
    for device in others:
        pl.semaphore_signal(barrier, inc=1, device_id=device, device_id_type=MESH)
    local = pltpu.make_async_copy(own, left.at[:, cols(core)], local_sem)
    local.start()

    for i in range(half_v // min(128, half_v)):
        m = min(128, half_v)
        line = eps_vir[:, pl.ds(pl.multiple_of(core * half_v + i * m, m), m)]
        eps_rows[pl.ds(i * m, m), :] = jnp.broadcast_to(line, (m, m)).T
    for b in range(BLOCKS):
        acc[b] = jnp.zeros((width, NC * k), jnp.float32)
    slot = start[0]
    occ_sum = eps_occ[slot + assignment[o]] + eps_occ[slot + assignment[o_prev]]
    eps_cols = [
        eps_vir[:, pl.ds(pl.multiple_of((x * NY + j) * width, width), width)] - occ_sum for j in range(NY)
    ]

    pl.semaphore_wait(barrier, len(others))

    def send_right(p):
        for d in range(NC):
            right_copy(p, d).start()

    left_copy().start()
    for p in range(min(AHEAD, parts)):
        send_right(p)
    local.wait()
    left_copy().wait_recv()

    def tile_block(p, x_):
        block = left[pl.ds(pl.multiple_of(x_ * NY * width, NY * width), NY * width), :]
        return dot(right[prds(p), :], block, ((1,), (1,)))

    def stage_tile(c):
        p = c // per_part

        @pl.when(lax.rem(c, per_part) == 0)
        def _():
            @pl.when(p + AHEAD < parts)
            def _():
                send_right(p + AHEAD)

            for s in range(NC):
                right_arrival(p, s).wait_recv()

            @pl.when(p >= first_last // PART)
            def _():
                right_last_copy(p).start()

            values = tile_block(p, x_far).astype(jnp.bfloat16)
            for j in range(NY):
                far_out[j, prds(p), :] = values[:, j * width : (j + 1) * width]

        for d in range(2):
            far_copy(c, d).start()

        @pl.when(lax.rem(c, per_part) == 0)
        def _():
            for x_ in (x_next, x_prev, x):
                values = tile_block(p, x_)
                for j in range(NY):
                    tile[x_ * NY + j, prds(p), :] = values[:, j * width : (j + 1) * width]

    def stage_near(c):
        for d in range(2):
            far_copy(c, d).wait_recv()
            x_ = (x_next, x_prev)[d]
            r = rds(c, half, d * half)
            for j in range(NY):
                tile[x_ * NY + j, r, :] += far[j, r, :].astype(jnp.float32)
            codes, unit = fixed([tile[x_ * NY + j, rds(c), :] for j in range(NY)])
            for j in range(NY):
                near_out[d, j, rds(c), :] = codes[j]
            near_unit_out[c, d] = jnp.broadcast_to(unit, near_unit_out.shape[2:])
            near_unit_copy(c, d).start()
            near_copy(c, d).start()

    def near_sum(c, y_):
        r = rds(c)
        total = tile[x * NY + y_, r, :]
        for d in range(2):
            total += near[d, y_, r, :].astype(jnp.float32) * near_unit[c, d][0:1, 0:1]
        return total

    def stage_sum(c):
        for d in range(2):
            near_unit_copy(c, d).wait_recv()
            near_copy(c, d).wait_recv()
        sums = [near_sum(c, j) for j in range(NY)]
        codes, unit = fixed(sums)
        for j in range(NY):
            tail_out[j, rds(c), :] = codes[j]
        tail_unit_out[c] = jnp.broadcast_to(unit, tail_unit_out.shape[1:])
        tail_unit_copy(c).start()
        tail_copy(c).start()
        for j in range(NY):
            tile[x * NY + j, rds(c), :] = sums[j]

    def stage_amp(c):
        tail_unit_copy(c).wait_recv()
        tail_copy(c).wait_recv()
        r = rds(c)
        for j in range(NY):
            total = tile[x * NY + j, r, :] + tail[j, r, :].astype(jnp.float32) * tail_unit[c][0:1, 0:1]
            denominator = eps_rows[r, 0:1] + eps_cols[j]
            amp[x * NY + j, r, :] = (total / denominator).astype(jnp.bfloat16)
        for d in range(2):
            amp_x_copy(c, d).start()

    def stage_forward(c):
        for d in range(2):
            amp_x_copy(c, d, (x_prev, x_next)[d]).wait_recv()
            amp_f_copy(c, d, (x_prev, x_next)[d]).start()

    def own_block(first, b):
        r = pl.ds(pl.multiple_of(first * rows, 16), GROUP)
        acc[b] += dot(amp[b, r, :], right[r, :], ((0,), (0,)))

    def stage_gamma(c):
        for d in range(2):
            amp_f_copy(c, d, x_far).wait_recv()

        @pl.when(c >= n - per_group)
        def _():
            amp_last_copy(c).start()

        @pl.when(lax.rem(c + 1, per_part) == 0)
        def _():
            p = c // per_part
            r = prds(p)
            total = dot(amp[0, r, :], left[pl.ds(0, width), :], ((1,), (0,)))
            for b in range(1, BLOCKS):
                total += dot(amp[b, r, :], left[pl.ds(b * width, width), :], ((1,), (0,)))
            back[r, :] = total.astype(jnp.bfloat16)
            for d in range(NC):
                back_copy(p, d).start()

        @pl.when((lax.rem(c + 1, per_group) == 0) & (c + 1 < n))
        def _():
            for b in range(BLOCKS):
                own_block(c + 1 - per_group, b)

            @pl.when(c + 1 == n - per_group)
            def _():
                for b in range(BLOCKS):
                    acc_copy(b).start()

    stages = (stage_tile, stage_gamma, stage_forward, stage_amp, stage_sum, stage_near)
    offsets = (0, 11, 9, 6, 3, 1)

    def tick(t, carry):
        for stage, offset in zip(stages, offsets):
            c = t - offset

            @pl.when((c >= 0) & (c < n))
            def _():
                stage(c)

        return carry

    lax.fori_loop(0, n + max(offsets), tick, 0)

    for p in range(first_last // PART, parts):
        right_last_copy(p).wait_recv()
    for c in range(n - per_group, n):
        amp_last_copy(c).wait_recv()
    for b in range(BLOCKS):
        acc_copy(b).wait_recv()

    last = pl.ds(first_last, GROUP)
    for b in range(BLOCKS):
        total = acc[b, :, cols(core)] + acc_in[b]
        total += dot(amp[b, last, :], right[last, cols(core)], ((0,), (0,)))
        total += dot(amp_last[b], right_last[...], ((0,), (0,)))
        out[pl.ds(b * width, width), :] = total

    def arrived(p, carry):
        for s in range(NC):
            back_arrival(p, s).wait_recv()
        return carry

    lax.fori_loop(0, parts, arrived, 0)
    for b in range(BLOCKS):
        r = pl.ds(b * width, width)
        out[r, :] += back_in[r, :].astype(jnp.float32)

    left_copy().wait_send()
    for b in range(BLOCKS):
        acc_copy(b).wait_send()
    for p in range(first_last // PART, parts):
        right_last_copy(p).wait_send()
    for c in range(n - per_group, n):
        amp_last_copy(c).wait_send()

    def part_sent(p, carry):
        for d in range(NC):
            right_copy(p, d).wait_send()
            back_copy(p, d).wait_send()
        return carry

    lax.fori_loop(0, parts, part_sent, 0)

    def sent(c, carry):
        for d in range(2):
            far_copy(c, d).wait_send()
            near_copy(c, d).wait_send()
            near_unit_copy(c, d).wait_send()
            amp_x_copy(c, d).wait_send()
            amp_f_copy(c, d, (x_prev, x_next)[d]).wait_send()
        tail_copy(c).wait_send()
        tail_unit_copy(c).wait_send()
        return carry

    lax.fori_loop(0, n, sent, 0)


def per_device(n_occ, rows, factors, eps_occ, eps_vir, window_start, assignment):
    own = factors[0]
    v, k = own.shape
    half_v, width = v // NC, v // BLOCKS
    n = half_v // rows
    f32, bf16 = jnp.float32, jnp.bfloat16
    dma = pltpu.SemaphoreType.DMA
    smem = pl.BlockSpec(memory_space=pltpu.SMEM)
    out = pl.pallas_call(
        functools.partial(kernel, n_occ, rows),
        out_shape=jax.ShapeDtypeStruct((v, k), f32),
        in_specs=[smem, smem, smem, pl.BlockSpec(memory_space=pl.ANY), pl.BlockSpec(memory_space=pltpu.VMEM)],
        out_specs=pl.BlockSpec(memory_space=pltpu.VMEM),
        scratch_shapes=[
            pltpu.VMEM((v, NC * k), bf16),
            pltpu.VMEM((half_v, NC * k), bf16),
            pltpu.VMEM((BLOCKS, half_v, width), f32),
            pltpu.VMEM((NY, half_v, width), bf16),
            pltpu.VMEM((NY, half_v, width), bf16),
            pltpu.VMEM((2, NY, half_v, width), jnp.int16),
            pltpu.VMEM((2, NY, half_v, width), jnp.int16),
            pltpu.VMEM((n, 2, 8, 128), f32),
            pltpu.VMEM((n, 2, 8, 128), f32),
            pltpu.VMEM((NY, half_v, width), jnp.int16),
            pltpu.VMEM((NY, half_v, width), jnp.int16),
            pltpu.VMEM((n, 8, 128), f32),
            pltpu.VMEM((n, 8, 128), f32),
            pltpu.VMEM((BLOCKS, half_v, width), bf16),
            pltpu.VMEM((BLOCKS, width, NC * k), f32),
            pltpu.VMEM((half_v, NC * k), bf16),
            pltpu.VMEM((v, k), bf16),
            pltpu.VMEM((BLOCKS, width, k), f32),
            pltpu.VMEM((half_v, min(128, half_v)), f32),
            pltpu.VMEM((GROUP, k), bf16),
            pltpu.VMEM((BLOCKS, GROUP, width), bf16),
            dma(()),
            dma((2,)),
            dma((half_v // PART, 2, 2)),
            dma((n, 2, 2)),
            dma((n, 2, 2)),
            dma((n, 2, 2)),
            dma((n, 2)),
            dma((n, 2)),
            dma((n, 2, 2)),
            dma((n, 2, 2)),
            dma((half_v // PART, 2, 2)),
            dma((BLOCKS, 2)),
            dma((GROUP // PART, 2)),
            dma((GROUP // rows, 2)),
        ],
        compiler_params=pltpu.CompilerParams(
            collective_id=0, has_side_effects=True, vmem_limit_bytes=60 * 2**20
        ),
        cost_estimate=pl.CostEstimate(
            flops=3 * 2 * v * v * k, bytes_accessed=6 * v * k, transcendentals=0
        ),
    )(eps_occ, window_start, assignment, own, eps_vir[None, :])
    return out[None]


def solution(mesh):
    in_specs = (P("occ", None, "aux"), P(), P(), P(), P())
    out_specs = P("occ", None, "aux")
    return jax.shard_map(
        functools.partial(per_device, mesh.shape["occ"], ROWS),
        mesh=mesh, in_specs=in_specs, out_specs=out_specs, check_vma=False,
    )
```

```python
import functools

import jax
import jax.numpy as jnp
from jax import lax
from jax.experimental import pallas as pl
from jax.experimental.pallas import tpu as pltpu
from jax.sharding import PartitionSpec as P

MESH = pl.DeviceIdType.MESH
NX, NY, NC = 4, 2, 2
BLOCKS = NX * NY
ROWS = 64
PART = 64
GROUP = 256
AHEAD = 4


def dot(a, b, dims):
    return lax.dot_general(a, b, (dims, ((), ())), preferred_element_type=jnp.float32)


def fixed(values):
    top = functools.reduce(jnp.maximum, [jnp.abs(v) for v in values])
    top = jnp.max(jnp.max(top, axis=0, keepdims=True), axis=1, keepdims=True)
    top = jnp.maximum(top, 1e-30)
    return [jnp.round(v * (32767.0 / top)).astype(jnp.int16) for v in values], top * (1 / 32767.0)


def kernel(
    n_occ, rows, eps_occ, start, assignment, own, eps_vir, out,
    left, right, tile, far_out, far, near_out, near, near_unit_out, near_unit,
    tail_out, tail, tail_unit_out, tail_unit, amp, acc, back, back_in, acc_in, eps_rows, right_last, amp_last,
    local_sem, left_sem, right_sem, far_sem, near_sem, near_unit_sem,
    tail_sem, tail_unit_sem,
    amp_x_sem, amp_f_sem, back_sem, acc_sem, right_last_sem, amp_last_sem,
):
    v, k = own.shape
    half_v = v // NC
    width = v // BLOCKS
    n = half_v // rows
    half = rows // 2
    per_part, per_group = PART // rows, GROUP // rows
    parts, first_last = half_v // PART, half_v - GROUP

    o = lax.axis_index("occ")
    u = lax.axis_index("aux")
    x, y, core = u // (NY * NC), (u // NC) % NY, u % NC
    o_next, o_prev = lax.rem(o + 1, n_occ), lax.rem(o + n_occ - 1, n_occ)
    x_next, x_prev, x_far = lax.rem(x + 1, NX), lax.rem(x + NX - 1, NX), lax.rem(x + 2, NX)

    def at(o_, x_, y_, c_):
        return (o_, (x_ * NY + y_) * NC + c_)

    sibling = at(o, x, y, 1 - core)
    partner = at(o, x, 1 - y, core)
    x_dev = (at(o, x_next, y, core), at(o, x_prev, y, core))
    next_dev = (at(o_next, x, y, 0), at(o_next, x, y, 1))
    prev_dev = (at(o_prev, x, y, 0), at(o_prev, x, y, 1))

    def remote(src, dst, sem, device, there=None):
        return pltpu.make_async_remote_copy(
            src_ref=src, dst_ref=dst, send_sem=sem.at[0], recv_sem=(sem if there is None else there).at[1],
            device_id=device, device_id_type=MESH,
        )

    def rds(c, size=rows, offset=0):
        return pl.ds(pl.multiple_of(c * rows + offset, 16), size)

    cols = lambda c_: pl.ds(pl.multiple_of(c_ * k, 128), k)
    pair_of = lambda x_: pl.ds(x_ * NY, NY)

    def left_copy():
        return remote(own, left.at[:, cols(core)], left_sem, sibling)

    def prds(p):
        return pl.ds(pl.multiple_of(p * PART, 16), PART)

    def right_copy(p, d):
        src = own.at[pl.ds(pl.multiple_of(d * half_v + p * PART, 16), PART), :]
        return remote(
            src, right.at[prds(p), cols(core)], right_sem.at[p, d], next_dev[d], right_sem.at[p, core]
        )

    def right_arrival(p, s):
        src = own.at[pl.ds(0, PART), :]
        return remote(src, right.at[prds(p), cols(s)], right_sem.at[p, s], next_dev[s])

    def right_last_copy(p):
        r = pl.ds(pl.multiple_of(p * PART - first_last, 16), PART)
        i = p - first_last // PART
        return remote(right.at[prds(p), cols(1 - core)], right_last.at[r, :], right_last_sem.at[i], sibling)

    def far_copy(c, d):
        r = rds(c, half, d * half)
        return remote(far_out.at[:, r, :], far.at[:, r, :], far_sem.at[c, d], x_dev[d])

    def near_copy(c, d):
        return remote(near_out.at[d, :, rds(c), :], near.at[d, :, rds(c), :], near_sem.at[c, d], x_dev[d])

    def near_unit_copy(c, d):
        return remote(near_unit_out.at[c, d], near_unit.at[c, d], near_unit_sem.at[c, d], x_dev[d])

    def tail_copy(c):
        return remote(tail_out.at[:, rds(c), :], tail.at[:, rds(c), :], tail_sem.at[c], partner)

    def tail_unit_copy(c):
        return remote(tail_unit_out.at[c], tail_unit.at[c], tail_unit_sem.at[c], partner)

    def amp_x_copy(c, d, x_=x):
        block = amp.at[pair_of(x_), rds(c), :]
        return remote(block, block, amp_x_sem.at[c, d], x_dev[d])

    def amp_f_copy(c, d, x_):
        block = amp.at[pair_of(x_), rds(c, half, d * half), :]
        return remote(block, block, amp_f_sem.at[c, d], x_dev[d])

    def amp_last_copy(c):
        r = pl.ds(pl.multiple_of(c * rows - first_last, 16), rows)
        return remote(amp.at[:, rds(c), :], amp_last.at[:, r, :], amp_last_sem.at[c - (n - per_group)], sibling)

    def back_copy(p, d):
        dst = back_in.at[pl.ds(pl.multiple_of(core * half_v + p * PART, 16), PART), :]
        return remote(back.at[prds(p), cols(d)], dst, back_sem.at[p, d], prev_dev[d], back_sem.at[p, core])

    def back_arrival(p, s):
        dst = back_in.at[pl.ds(pl.multiple_of(s * half_v + p * PART, 16), PART), :]
        return remote(back.at[prds(p), cols(s)], dst, back_sem.at[p, s], prev_dev[s])

    def acc_copy(b):
        return remote(acc.at[b, :, cols(1 - core)], acc_in.at[b], acc_sem.at[b], sibling)

    barrier = pltpu.get_barrier_semaphore()
    others = (sibling, partner) + x_dev + next_dev + prev_dev
    for device in others:
        pl.semaphore_signal(barrier, inc=1, device_id=device, device_id_type=MESH)
    local = pltpu.make_async_copy(own, left.at[:, cols(core)], local_sem)
    local.start()

    for i in range(half_v // min(128, half_v)):
        m = min(128, half_v)
        line = eps_vir[:, pl.ds(pl.multiple_of(core * half_v + i * m, m), m)]
        eps_rows[pl.ds(i * m, m), :] = jnp.broadcast_to(line, (m, m)).T
    for b in range(BLOCKS):
        acc[b] = jnp.zeros((width, NC * k), jnp.float32)
    slot = start[0]
    occ_sum = eps_occ[slot + assignment[o]] + eps_occ[slot + assignment[o_prev]]
    eps_cols = [
        eps_vir[:, pl.ds(pl.multiple_of((x * NY + j) * width, width), width)] - occ_sum for j in range(NY)
    ]

    pl.semaphore_wait(barrier, len(others))

    def send_right(p):
        for d in range(NC):
            right_copy(p, d).start()

    left_copy().start()
    for p in range(min(AHEAD, parts)):
        send_right(p)
    local.wait()
    left_copy().wait_recv()

    def tile_block(p, x_):
        block = left[pl.ds(pl.multiple_of(x_ * NY * width, NY * width), NY * width), :]
        return dot(right[prds(p), :], block, ((1,), (1,)))

    def stage_tile(c):
        p = c // per_part

        @pl.when(lax.rem(c, per_part) == 0)
        def _():
            @pl.when(p + AHEAD < parts)
            def _():
                send_right(p + AHEAD)

            for s in range(NC):
                right_arrival(p, s).wait_recv()

            @pl.when(p >= first_last // PART)
            def _():
                right_last_copy(p).start()

            values = tile_block(p, x_far).astype(jnp.bfloat16)
            for j in range(NY):
                far_out[j, prds(p), :] = values[:, j * width : (j + 1) * width]

        for d in range(2):
            far_copy(c, d).start()

        @pl.when(lax.rem(c, per_part) == 0)
        def _():
            for x_ in (x_next, x_prev, x):
                values = tile_block(p, x_)
                for j in range(NY):
                    tile[x_ * NY + j, prds(p), :] = values[:, j * width : (j + 1) * width]

    def stage_near(c):
        for d in range(2):
            far_copy(c, d).wait_recv()
            x_ = (x_next, x_prev)[d]
            r = rds(c, half, d * half)
            for j in range(NY):
                tile[x_ * NY + j, r, :] += far[j, r, :].astype(jnp.float32)
            codes, unit = fixed([tile[x_ * NY + j, rds(c), :] for j in range(NY)])
            for j in range(NY):
                near_out[d, j, rds(c), :] = codes[j]
            near_unit_out[c, d] = jnp.broadcast_to(unit, near_unit_out.shape[2:])
            near_unit_copy(c, d).start()
            near_copy(c, d).start()

    def near_sum(c, y_):
        r = rds(c)
        total = tile[x * NY + y_, r, :]
        for d in range(2):
            total += near[d, y_, r, :].astype(jnp.float32) * near_unit[c, d][0:1, 0:1]
        return total

    def stage_sum(c):
        for d in range(2):
            near_unit_copy(c, d).wait_recv()
            near_copy(c, d).wait_recv()
        sums = [near_sum(c, j) for j in range(NY)]
        codes, unit = fixed(sums)
        for j in range(NY):
            tail_out[j, rds(c), :] = codes[j]
        tail_unit_out[c] = jnp.broadcast_to(unit, tail_unit_out.shape[1:])
        tail_unit_copy(c).start()
        tail_copy(c).start()
        for j in range(NY):
            tile[x * NY + j, rds(c), :] = sums[j]

    def stage_amp(c):
        tail_unit_copy(c).wait_recv()
        tail_copy(c).wait_recv()
        r = rds(c)
        for j in range(NY):
            total = tile[x * NY + j, r, :] + tail[j, r, :].astype(jnp.float32) * tail_unit[c][0:1, 0:1]
            denominator = eps_rows[r, 0:1] + eps_cols[j]
            amp[x * NY + j, r, :] = (total / denominator).astype(jnp.bfloat16)
        for d in range(2):
            amp_x_copy(c, d).start()

    def stage_forward(c):
        for d in range(2):
            amp_x_copy(c, d, (x_prev, x_next)[d]).wait_recv()
            amp_f_copy(c, d, (x_prev, x_next)[d]).start()

    def own_block(first, b):
        r = pl.ds(pl.multiple_of(first * rows, 16), GROUP)
        acc[b] += dot(amp[b, r, :], right[r, :], ((0,), (0,)))

    def stage_gamma(c):
        for d in range(2):
            amp_f_copy(c, d, x_far).wait_recv()

        @pl.when(c >= n - per_group)
        def _():
            amp_last_copy(c).start()

        @pl.when(lax.rem(c + 1, per_part) == 0)
        def _():
            p = c // per_part
            r = prds(p)
            total = dot(amp[0, r, :], left[pl.ds(0, width), :], ((1,), (0,)))
            for b in range(1, BLOCKS):
                total += dot(amp[b, r, :], left[pl.ds(b * width, width), :], ((1,), (0,)))
            back[r, :] = total.astype(jnp.bfloat16)
            for d in range(NC):
                back_copy(p, d).start()

        @pl.when((lax.rem(c + 1, per_group) == 0) & (c + 1 < n))
        def _():
            for b in range(BLOCKS):
                own_block(c + 1 - per_group, b)

            @pl.when(c + 1 == n - per_group)
            def _():
                for b in range(BLOCKS):
                    acc_copy(b).start()

    stages = (stage_tile, stage_gamma, stage_forward, stage_amp, stage_sum, stage_near)
    offsets = (0, 14, 11, 8, 5, 2)

    def tick(t, carry):
        for stage, offset in zip(stages, offsets):
            c = t - offset

            @pl.when((c >= 0) & (c < n))
            def _():
                stage(c)

        return carry

    lax.fori_loop(0, n + max(offsets), tick, 0)

    for p in range(first_last // PART, parts):
        right_last_copy(p).wait_recv()
    for c in range(n - per_group, n):
        amp_last_copy(c).wait_recv()
    for b in range(BLOCKS):
        acc_copy(b).wait_recv()

    last = pl.ds(first_last, GROUP)
    for b in range(BLOCKS):
        total = acc[b, :, cols(core)] + acc_in[b]
        total += dot(amp[b, last, :], right[last, cols(core)], ((0,), (0,)))
        total += dot(amp_last[b], right_last[...], ((0,), (0,)))
        out[pl.ds(b * width, width), :] = total

    def arrived(p, carry):
        for s in range(NC):
            back_arrival(p, s).wait_recv()
        return carry

    lax.fori_loop(0, parts, arrived, 0)
    for b in range(BLOCKS):
        r = pl.ds(b * width, width)
        out[r, :] += back_in[r, :].astype(jnp.float32)

    left_copy().wait_send()
    for b in range(BLOCKS):
        acc_copy(b).wait_send()
    for p in range(first_last // PART, parts):
        right_last_copy(p).wait_send()
    for c in range(n - per_group, n):
        amp_last_copy(c).wait_send()

    def part_sent(p, carry):
        for d in range(NC):
            right_copy(p, d).wait_send()
            back_copy(p, d).wait_send()
        return carry

    lax.fori_loop(0, parts, part_sent, 0)

    def sent(c, carry):
        for d in range(2):
            far_copy(c, d).wait_send()
            near_copy(c, d).wait_send()
            near_unit_copy(c, d).wait_send()
            amp_x_copy(c, d).wait_send()
            amp_f_copy(c, d, (x_prev, x_next)[d]).wait_send()
        tail_copy(c).wait_send()
        tail_unit_copy(c).wait_send()
        return carry

    lax.fori_loop(0, n, sent, 0)


def per_device(n_occ, rows, factors, eps_occ, eps_vir, window_start, assignment):
    own = factors[0]
    v, k = own.shape
    half_v, width = v // NC, v // BLOCKS
    n = half_v // rows
    f32, bf16 = jnp.float32, jnp.bfloat16
    dma = pltpu.SemaphoreType.DMA
    smem = pl.BlockSpec(memory_space=pltpu.SMEM)
    out = pl.pallas_call(
        functools.partial(kernel, n_occ, rows),
        out_shape=jax.ShapeDtypeStruct((v, k), f32),
        in_specs=[smem, smem, smem, pl.BlockSpec(memory_space=pl.ANY), pl.BlockSpec(memory_space=pltpu.VMEM)],
        out_specs=pl.BlockSpec(memory_space=pltpu.VMEM),
        scratch_shapes=[
            pltpu.VMEM((v, NC * k), bf16),
            pltpu.VMEM((half_v, NC * k), bf16),
            pltpu.VMEM((BLOCKS, half_v, width), f32),
            pltpu.VMEM((NY, half_v, width), bf16),
            pltpu.VMEM((NY, half_v, width), bf16),
            pltpu.VMEM((2, NY, half_v, width), jnp.int16),
            pltpu.VMEM((2, NY, half_v, width), jnp.int16),
            pltpu.VMEM((n, 2, 8, 128), f32),
            pltpu.VMEM((n, 2, 8, 128), f32),
            pltpu.VMEM((NY, half_v, width), jnp.int16),
            pltpu.VMEM((NY, half_v, width), jnp.int16),
            pltpu.VMEM((n, 8, 128), f32),
            pltpu.VMEM((n, 8, 128), f32),
            pltpu.VMEM((BLOCKS, half_v, width), bf16),
            pltpu.VMEM((BLOCKS, width, NC * k), f32),
            pltpu.VMEM((half_v, NC * k), bf16),
            pltpu.VMEM((v, k), bf16),
            pltpu.VMEM((BLOCKS, width, k), f32),
            pltpu.VMEM((half_v, min(128, half_v)), f32),
            pltpu.VMEM((GROUP, k), bf16),
            pltpu.VMEM((BLOCKS, GROUP, width), bf16),
            dma(()),
            dma((2,)),
            dma((half_v // PART, 2, 2)),
            dma((n, 2, 2)),
            dma((n, 2, 2)),
            dma((n, 2, 2)),
            dma((n, 2)),
            dma((n, 2)),
            dma((n, 2, 2)),
            dma((n, 2, 2)),
            dma((half_v // PART, 2, 2)),
            dma((BLOCKS, 2)),
            dma((GROUP // PART, 2)),
            dma((GROUP // rows, 2)),
        ],
        compiler_params=pltpu.CompilerParams(
            collective_id=0, has_side_effects=True, vmem_limit_bytes=60 * 2**20
        ),
        cost_estimate=pl.CostEstimate(
            flops=3 * 2 * v * v * k, bytes_accessed=6 * v * k, transcendentals=0
        ),
    )(eps_occ, window_start, assignment, own, eps_vir[None, :])
    return out[None]


def solution(mesh):
    in_specs = (P("occ", None, "aux"), P(), P(), P(), P())
    out_specs = P("occ", None, "aux")
    return jax.shard_map(
        functools.partial(per_device, mesh.shape["occ"], ROWS),
        mesh=mesh, in_specs=in_specs, out_specs=out_specs, check_vma=False,
    )
```

```python
import functools

import jax
import jax.numpy as jnp
from jax import lax
from jax.experimental import pallas as pl
from jax.experimental.pallas import tpu as pltpu
from jax.sharding import PartitionSpec as P

MESH = pl.DeviceIdType.MESH
NX, NY, NC = 4, 2, 2
BLOCKS = NX * NY
Y_LO, Y_ALL = 2, 4
ROWS = 64
PART = 64
GROUP = 256
AHEAD = 4


def dot(a, b, dims):
    return lax.dot_general(a, b, (dims, ((), ())), preferred_element_type=jnp.float32)


def fixed(values):
    top = functools.reduce(jnp.maximum, [jnp.abs(v) for v in values])
    top = jnp.max(jnp.max(top, axis=0, keepdims=True), axis=1, keepdims=True)
    top = jnp.maximum(top, 1e-30)
    return [jnp.round(v * (32767.0 / top)).astype(jnp.int16) for v in values], top * (1 / 32767.0)


def kernel(
    n_occ, rows, eps_occ, start, assignment, own, eps_vir, out,
    left, right, tile, far_out, far, near_out, near, near_unit_out, near_unit,
    tail_out, tail, tail_unit_out, tail_unit, tail_via, tail_unit_via, amp, acc, back, back_in, acc_in, eps_rows, right_last, amp_last,
    local_sem, left_sem, right_sem, far_sem, near_sem, near_unit_sem,
    tail_sem, tail_unit_sem, tail_via_sem, tail_unit_via_sem,
    amp_x_sem, amp_f_sem, back_sem, acc_sem, right_last_sem, amp_last_sem,
):
    v, k = own.shape
    half_v = v // NC
    width = v // BLOCKS
    n = half_v // rows
    half = rows // 2
    per_part, per_group = PART // rows, GROUP // rows
    parts, first_last = half_v // PART, half_v - GROUP

    o = lax.axis_index("occ")
    u = lax.axis_index("aux")
    x, y, core = u // (NY * NC), (u // NC) % NY, u % NC
    o_next, o_prev = lax.rem(o + 1, n_occ), lax.rem(o + n_occ - 1, n_occ)
    x_next, x_prev, x_far = lax.rem(x + 1, NX), lax.rem(x + NX - 1, NX), lax.rem(x + 2, NX)

    def at(o_, x_, y_, c_):
        return (o_, (x_ * NY + y_) * NC + c_)

    sibling = at(o, x, y, 1 - core)
    def across(step):
        place = lax.rem(y * Y_LO + lax.rem(o, Y_LO) + step + Y_ALL, Y_ALL)
        return at((o // Y_LO) * Y_LO + lax.rem(place, Y_LO), x, place // Y_LO, core)

    hop, hop_back = across(1 - 2 * core), across(2 * core - 1)
    x_dev = (at(o, x_next, y, core), at(o, x_prev, y, core))
    next_dev = (at(o_next, x, y, 0), at(o_next, x, y, 1))
    prev_dev = (at(o_prev, x, y, 0), at(o_prev, x, y, 1))

    def remote(src, dst, sem, device, there=None):
        return pltpu.make_async_remote_copy(
            src_ref=src, dst_ref=dst, send_sem=sem.at[0], recv_sem=(sem if there is None else there).at[1],
            device_id=device, device_id_type=MESH,
        )

    def rds(c, size=rows, offset=0):
        return pl.ds(pl.multiple_of(c * rows + offset, 16), size)

    cols = lambda c_: pl.ds(pl.multiple_of(c_ * k, 128), k)
    pair_of = lambda x_: pl.ds(x_ * NY, NY)

    def left_copy():
        return remote(own, left.at[:, cols(core)], left_sem, sibling)

    def prds(p):
        return pl.ds(pl.multiple_of(p * PART, 16), PART)

    def right_copy(p, d):
        src = own.at[pl.ds(pl.multiple_of(d * half_v + p * PART, 16), PART), :]
        return remote(
            src, right.at[prds(p), cols(core)], right_sem.at[p, d], next_dev[d], right_sem.at[p, core]
        )

    def right_arrival(p, s):
        src = own.at[pl.ds(0, PART), :]
        return remote(src, right.at[prds(p), cols(s)], right_sem.at[p, s], next_dev[s])

    def right_last_copy(p):
        r = pl.ds(pl.multiple_of(p * PART - first_last, 16), PART)
        i = p - first_last // PART
        return remote(right.at[prds(p), cols(1 - core)], right_last.at[r, :], right_last_sem.at[i], sibling)

    def far_copy(c, d):
        r = rds(c, half, d * half)
        return remote(far_out.at[:, r, :], far.at[:, r, :], far_sem.at[c, d], x_dev[d])

    def near_copy(c, d):
        return remote(near_out.at[d, :, rds(c), :], near.at[d, :, rds(c), :], near_sem.at[c, d], x_dev[d])

    def near_unit_copy(c, d):
        return remote(near_unit_out.at[c, d], near_unit.at[c, d], near_unit_sem.at[c, d], x_dev[d])

    def tail_copy(c):
        return remote(tail_out.at[:, rds(c), :], tail_via.at[:, rds(c), :], tail_via_sem.at[c], hop)

    def tail_unit_copy(c):
        return remote(tail_unit_out.at[c], tail_unit_via.at[c], tail_unit_via_sem.at[c], hop)

    def tail_pass(c):
        return remote(tail_via.at[:, rds(c), :], tail.at[:, rds(c), :], tail_sem.at[c], hop)

    def tail_unit_pass(c):
        return remote(tail_unit_via.at[c], tail_unit.at[c], tail_unit_sem.at[c], hop)

    def amp_x_copy(c, d, x_=x):
        block = amp.at[pair_of(x_), rds(c), :]
        return remote(block, block, amp_x_sem.at[c, d], x_dev[d])

    def amp_f_copy(c, d, x_):
        block = amp.at[pair_of(x_), rds(c, half, d * half), :]
        return remote(block, block, amp_f_sem.at[c, d], x_dev[d])

    def amp_last_copy(c):
        r = pl.ds(pl.multiple_of(c * rows - first_last, 16), rows)
        return remote(amp.at[:, rds(c), :], amp_last.at[:, r, :], amp_last_sem.at[c - (n - per_group)], sibling)

    def back_copy(p, d):
        dst = back_in.at[pl.ds(pl.multiple_of(core * half_v + p * PART, 16), PART), :]
        return remote(back.at[prds(p), cols(d)], dst, back_sem.at[p, d], prev_dev[d], back_sem.at[p, core])

    def back_arrival(p, s):
        dst = back_in.at[pl.ds(pl.multiple_of(s * half_v + p * PART, 16), PART), :]
        return remote(back.at[prds(p), cols(s)], dst, back_sem.at[p, s], prev_dev[s])

    def acc_copy(b):
        return remote(acc.at[b, :, cols(1 - core)], acc_in.at[b], acc_sem.at[b], sibling)

    barrier = pltpu.get_barrier_semaphore()
    others = (sibling, hop, hop_back) + x_dev + next_dev + prev_dev
    for device in others:
        pl.semaphore_signal(barrier, inc=1, device_id=device, device_id_type=MESH)
    local = pltpu.make_async_copy(own, left.at[:, cols(core)], local_sem)
    local.start()

    for i in range(half_v // min(128, half_v)):
        m = min(128, half_v)
        line = eps_vir[:, pl.ds(pl.multiple_of(core * half_v + i * m, m), m)]
        eps_rows[pl.ds(i * m, m), :] = jnp.broadcast_to(line, (m, m)).T
    for b in range(BLOCKS):
        acc[b] = jnp.zeros((width, NC * k), jnp.float32)
    slot = start[0]
    occ_sum = eps_occ[slot + assignment[o]] + eps_occ[slot + assignment[o_prev]]
    eps_cols = [
        eps_vir[:, pl.ds(pl.multiple_of((x * NY + j) * width, width), width)] - occ_sum for j in range(NY)
    ]

    pl.semaphore_wait(barrier, len(others))

    def send_right(p):
        for d in range(NC):
            right_copy(p, d).start()

    left_copy().start()
    for p in range(min(AHEAD, parts)):
        send_right(p)
    local.wait()
    left_copy().wait_recv()

    def tile_block(p, x_):
        block = left[pl.ds(pl.multiple_of(x_ * NY * width, NY * width), NY * width), :]
        return dot(right[prds(p), :], block, ((1,), (1,)))

    def stage_tile(c):
        p = c // per_part

        @pl.when(lax.rem(c, per_part) == 0)
        def _():
            @pl.when(p + AHEAD < parts)
            def _():
                send_right(p + AHEAD)

            for s in range(NC):
                right_arrival(p, s).wait_recv()

            @pl.when(p >= first_last // PART)
            def _():
                right_last_copy(p).start()

            values = tile_block(p, x_far).astype(jnp.bfloat16)
            for j in range(NY):
                far_out[j, prds(p), :] = values[:, j * width : (j + 1) * width]

        for d in range(2):
            far_copy(c, d).start()

        @pl.when(lax.rem(c, per_part) == 0)
        def _():
            for x_ in (x_next, x_prev, x):
                values = tile_block(p, x_)
                for j in range(NY):
                    tile[x_ * NY + j, prds(p), :] = values[:, j * width : (j + 1) * width]

    def stage_near(c):
        for d in range(2):
            far_copy(c, d).wait_recv()
            x_ = (x_next, x_prev)[d]
            r = rds(c, half, d * half)
            for j in range(NY):
                tile[x_ * NY + j, r, :] += far[j, r, :].astype(jnp.float32)
            codes, unit = fixed([tile[x_ * NY + j, rds(c), :] for j in range(NY)])
            for j in range(NY):
                near_out[d, j, rds(c), :] = codes[j]
            near_unit_out[c, d] = jnp.broadcast_to(unit, near_unit_out.shape[2:])
            near_unit_copy(c, d).start()
            near_copy(c, d).start()

    def near_sum(c, y_):
        r = rds(c)
        total = tile[x * NY + y_, r, :]
        for d in range(2):
            total += near[d, y_, r, :].astype(jnp.float32) * near_unit[c, d][0:1, 0:1]
        return total

    def stage_sum(c):
        for d in range(2):
            near_unit_copy(c, d).wait_recv()
            near_copy(c, d).wait_recv()
        sums = [near_sum(c, j) for j in range(NY)]
        codes, unit = fixed(sums)
        for j in range(NY):
            tail_out[j, rds(c), :] = codes[j]
        tail_unit_out[c] = jnp.broadcast_to(unit, tail_unit_out.shape[1:])
        tail_unit_copy(c).start()
        tail_copy(c).start()
        for j in range(NY):
            tile[x * NY + j, rds(c), :] = sums[j]

    def stage_tail(c):
        tail_unit_copy(c).wait_recv()
        tail_unit_pass(c).start()
        tail_copy(c).wait_recv()
        tail_pass(c).start()

    def stage_amp(c):
        tail_unit_pass(c).wait_recv()
        tail_pass(c).wait_recv()
        r = rds(c)
        for j in range(NY):
            total = tile[x * NY + j, r, :] + tail[j, r, :].astype(jnp.float32) * tail_unit[c][0:1, 0:1]
            denominator = eps_rows[r, 0:1] + eps_cols[j]
            amp[x * NY + j, r, :] = (total / denominator).astype(jnp.bfloat16)
        for d in range(2):
            amp_x_copy(c, d).start()

    def stage_forward(c):
        for d in range(2):
            amp_x_copy(c, d, (x_prev, x_next)[d]).wait_recv()
            amp_f_copy(c, d, (x_prev, x_next)[d]).start()

    def own_block(first, b):
        r = pl.ds(pl.multiple_of(first * rows, 16), GROUP)
        acc[b] += dot(amp[b, r, :], right[r, :], ((0,), (0,)))

    def stage_gamma(c):
        for d in range(2):
            amp_f_copy(c, d, x_far).wait_recv()

        @pl.when(c >= n - per_group)
        def _():
            amp_last_copy(c).start()

        @pl.when(lax.rem(c + 1, per_part) == 0)
        def _():
            p = c // per_part
            r = prds(p)
            total = dot(amp[0, r, :], left[pl.ds(0, width), :], ((1,), (0,)))
            for b in range(1, BLOCKS):
                total += dot(amp[b, r, :], left[pl.ds(b * width, width), :], ((1,), (0,)))
            back[r, :] = total.astype(jnp.bfloat16)
            for d in range(NC):
                back_copy(p, d).start()

        @pl.when((lax.rem(c + 1, per_group) == 0) & (c + 1 < n))
        def _():
            for b in range(BLOCKS):
                own_block(c + 1 - per_group, b)

            @pl.when(c + 1 == n - per_group)
            def _():
                for b in range(BLOCKS):
                    acc_copy(b).start()

    stages = (stage_tile, stage_gamma, stage_forward, stage_amp, stage_tail, stage_sum, stage_near)
    offsets = (0, 15, 12, 9, 6, 4, 2)

    def tick(t, carry):
        for stage, offset in zip(stages, offsets):
            c = t - offset

            @pl.when((c >= 0) & (c < n))
            def _():
                stage(c)

        return carry

    lax.fori_loop(0, n + max(offsets), tick, 0)

    for p in range(first_last // PART, parts):
        right_last_copy(p).wait_recv()
    for c in range(n - per_group, n):
        amp_last_copy(c).wait_recv()
    for b in range(BLOCKS):
        acc_copy(b).wait_recv()

    last = pl.ds(first_last, GROUP)
    for b in range(BLOCKS):
        total = acc[b, :, cols(core)] + acc_in[b]
        total += dot(amp[b, last, :], right[last, cols(core)], ((0,), (0,)))
        total += dot(amp_last[b], right_last[...], ((0,), (0,)))
        out[pl.ds(b * width, width), :] = total

    def arrived(p, carry):
        for s in range(NC):
            back_arrival(p, s).wait_recv()
        return carry

    lax.fori_loop(0, parts, arrived, 0)
    for b in range(BLOCKS):
        r = pl.ds(b * width, width)
        out[r, :] += back_in[r, :].astype(jnp.float32)

    left_copy().wait_send()
    for b in range(BLOCKS):
        acc_copy(b).wait_send()
    for p in range(first_last // PART, parts):
        right_last_copy(p).wait_send()
    for c in range(n - per_group, n):
        amp_last_copy(c).wait_send()

    def part_sent(p, carry):
        for d in range(NC):
            right_copy(p, d).wait_send()
            back_copy(p, d).wait_send()
        return carry

    lax.fori_loop(0, parts, part_sent, 0)

    def sent(c, carry):
        for d in range(2):
            far_copy(c, d).wait_send()
            near_copy(c, d).wait_send()
            near_unit_copy(c, d).wait_send()
            amp_x_copy(c, d).wait_send()
            amp_f_copy(c, d, (x_prev, x_next)[d]).wait_send()
        tail_copy(c).wait_send()
        tail_unit_copy(c).wait_send()
        tail_pass(c).wait_send()
        tail_unit_pass(c).wait_send()
        return carry

    lax.fori_loop(0, n, sent, 0)


def per_device(n_occ, rows, factors, eps_occ, eps_vir, window_start, assignment):
    own = factors[0]
    v, k = own.shape
    half_v, width = v // NC, v // BLOCKS
    n = half_v // rows
    f32, bf16 = jnp.float32, jnp.bfloat16
    dma = pltpu.SemaphoreType.DMA
    smem = pl.BlockSpec(memory_space=pltpu.SMEM)
    out = pl.pallas_call(
        functools.partial(kernel, n_occ, rows),
        out_shape=jax.ShapeDtypeStruct((v, k), f32),
        in_specs=[smem, smem, smem, pl.BlockSpec(memory_space=pl.ANY), pl.BlockSpec(memory_space=pltpu.VMEM)],
        out_specs=pl.BlockSpec(memory_space=pltpu.VMEM),
        scratch_shapes=[
            pltpu.VMEM((v, NC * k), bf16),
            pltpu.VMEM((half_v, NC * k), bf16),
            pltpu.VMEM((BLOCKS, half_v, width), f32),
            pltpu.VMEM((NY, half_v, width), bf16),
            pltpu.VMEM((NY, half_v, width), bf16),
            pltpu.VMEM((2, NY, half_v, width), jnp.int16),
            pltpu.VMEM((2, NY, half_v, width), jnp.int16),
            pltpu.VMEM((n, 2, 8, 128), f32),
            pltpu.VMEM((n, 2, 8, 128), f32),
            pltpu.VMEM((NY, half_v, width), jnp.int16),
            pltpu.VMEM((NY, half_v, width), jnp.int16),
            pltpu.VMEM((n, 8, 128), f32),
            pltpu.VMEM((n, 8, 128), f32),
            pltpu.VMEM((NY, half_v, width), jnp.int16),
            pltpu.VMEM((n, 8, 128), f32),
            pltpu.VMEM((BLOCKS, half_v, width), bf16),
            pltpu.VMEM((BLOCKS, width, NC * k), f32),
            pltpu.VMEM((half_v, NC * k), bf16),
            pltpu.VMEM((v, k), bf16),
            pltpu.VMEM((BLOCKS, width, k), f32),
            pltpu.VMEM((half_v, min(128, half_v)), f32),
            pltpu.VMEM((GROUP, k), bf16),
            pltpu.VMEM((BLOCKS, GROUP, width), bf16),
            dma(()),
            dma((2,)),
            dma((half_v // PART, 2, 2)),
            dma((n, 2, 2)),
            dma((n, 2, 2)),
            dma((n, 2, 2)),
            dma((n, 2)),
            dma((n, 2)),
            dma((n, 2)),
            dma((n, 2)),
            dma((n, 2, 2)),
            dma((n, 2, 2)),
            dma((half_v // PART, 2, 2)),
            dma((BLOCKS, 2)),
            dma((GROUP // PART, 2)),
            dma((GROUP // rows, 2)),
        ],
        compiler_params=pltpu.CompilerParams(
            collective_id=0, has_side_effects=True, vmem_limit_bytes=60 * 2**20
        ),
        cost_estimate=pl.CostEstimate(
            flops=3 * 2 * v * v * k, bytes_accessed=6 * v * k, transcendentals=0
        ),
    )(eps_occ, window_start, assignment, own, eps_vir[None, :])
    return out[None]


def solution(mesh):
    in_specs = (P("occ", None, "aux"), P(), P(), P(), P())
    out_specs = P("occ", None, "aux")
    return jax.shard_map(
        functools.partial(per_device, mesh.shape["occ"], ROWS),
        mesh=mesh, in_specs=in_specs, out_specs=out_specs, check_vma=False,
    )
```

```python
import functools

import jax
import jax.numpy as jnp
from jax import lax
from jax.experimental import pallas as pl
from jax.experimental.pallas import tpu as pltpu
from jax.sharding import PartitionSpec as P

MESH = pl.DeviceIdType.MESH
NX, NY, NC = 4, 2, 2
BLOCKS = NX * NY
ROWS = 64
PART = 128
GROUP = 256
AHEAD = 2


def dot(a, b, dims):
    return lax.dot_general(a, b, (dims, ((), ())), preferred_element_type=jnp.float32)


def fixed(values):
    top = functools.reduce(jnp.maximum, [jnp.abs(v) for v in values])
    top = jnp.max(jnp.max(top, axis=0, keepdims=True), axis=1, keepdims=True)
    top = jnp.maximum(top, 1e-30)
    return [jnp.round(v * (32767.0 / top)).astype(jnp.int16) for v in values], top * (1 / 32767.0)


def kernel(
    n_occ, rows, eps_occ, start, assignment, own, eps_vir, out,
    left, right, tile, far_out, far, near_out, near, near_unit_out, near_unit,
    tail_out, tail, tail_unit_out, tail_unit, amp, acc, back, back_in, acc_in, eps_rows, right_last, amp_last,
    local_sem, left_sem, right_sem, far_sem, near_sem, near_unit_sem,
    tail_sem, tail_unit_sem,
    amp_y_sem, amp_x_sem, amp_f_sem, back_sem, acc_sem, right_last_sem, amp_last_sem,
):
    v, k = own.shape
    half_v = v // NC
    width = v // BLOCKS
    n = half_v // rows
    half = rows // 2
    per_part, per_group = PART // rows, GROUP // rows
    parts, first_last = half_v // PART, half_v - GROUP

    o = lax.axis_index("occ")
    u = lax.axis_index("aux")
    x, y, core = u // (NY * NC), (u // NC) % NY, u % NC
    o_next, o_prev = lax.rem(o + 1, n_occ), lax.rem(o + n_occ - 1, n_occ)
    x_next, x_prev, x_far = lax.rem(x + 1, NX), lax.rem(x + NX - 1, NX), lax.rem(x + 2, NX)

    def at(o_, x_, y_, c_):
        return (o_, (x_ * NY + y_) * NC + c_)

    sibling = at(o, x, y, 1 - core)
    partner = at(o, x, 1 - y, core)
    x_dev = (at(o, x_next, y, core), at(o, x_prev, y, core))
    next_dev = (at(o_next, x, y, 0), at(o_next, x, y, 1))
    prev_dev = (at(o_prev, x, y, 0), at(o_prev, x, y, 1))
    mine, theirs = x * NY + y, x * NY + 1 - y

    def remote(src, dst, sem, device, there=None):
        return pltpu.make_async_remote_copy(
            src_ref=src, dst_ref=dst, send_sem=sem.at[0], recv_sem=(sem if there is None else there).at[1],
            device_id=device, device_id_type=MESH,
        )

    def rds(c, size=rows, offset=0):
        return pl.ds(pl.multiple_of(c * rows + offset, 16), size)

    cols = lambda c_: pl.ds(pl.multiple_of(c_ * k, 128), k)
    pair_of = lambda x_: pl.ds(x_ * NY, NY)

    def left_copy():
        return remote(own, left.at[:, cols(core)], left_sem, sibling)

    def prds(p):
        return pl.ds(pl.multiple_of(p * PART, 16), PART)

    def right_copy(p, d):
        src = own.at[pl.ds(pl.multiple_of(d * half_v + p * PART, 16), PART), :]
        return remote(
            src, right.at[prds(p), cols(core)], right_sem.at[p, d], next_dev[d], right_sem.at[p, core]
        )

    def right_arrival(p, s):
        src = own.at[pl.ds(0, PART), :]
        return remote(src, right.at[prds(p), cols(s)], right_sem.at[p, s], next_dev[s])

    def right_last_copy(p):
        r = pl.ds(pl.multiple_of(p * PART - first_last, 16), PART)
        i = p - first_last // PART
        return remote(right.at[prds(p), cols(1 - core)], right_last.at[r, :], right_last_sem.at[i], sibling)

    def far_copy(c, d):
        r = rds(c, half, d * half)
        return remote(far_out.at[:, r, :], far.at[:, r, :], far_sem.at[c, d], x_dev[d])

    def near_copy(c, d):
        return remote(near_out.at[d, :, rds(c), :], near.at[d, :, rds(c), :], near_sem.at[c, d], x_dev[d])

    def near_unit_copy(c, d):
        return remote(near_unit_out.at[c, d], near_unit.at[c, d], near_unit_sem.at[c, d], x_dev[d])

    def tail_copy(c):
        return remote(tail_out.at[rds(c), :], tail.at[rds(c), :], tail_sem.at[c], partner)

    def tail_unit_copy(c):
        return remote(tail_unit_out.at[c], tail_unit.at[c], tail_unit_sem.at[c], partner)

    def amp_y_copy(c, block=mine):
        block = amp.at[block, rds(c), :]
        return remote(block, block, amp_y_sem.at[c], partner)

    def amp_x_copy(c, d, x_=x):
        block = amp.at[pair_of(x_), rds(c), :]
        return remote(block, block, amp_x_sem.at[c, d], x_dev[d])

    def amp_f_copy(c, d, x_):
        block = amp.at[pair_of(x_), rds(c, half, d * half), :]
        return remote(block, block, amp_f_sem.at[c, d], x_dev[d])

    def amp_last_copy(c):
        r = pl.ds(pl.multiple_of(c * rows - first_last, 16), rows)
        return remote(amp.at[:, rds(c), :], amp_last.at[:, r, :], amp_last_sem.at[c - (n - per_group)], sibling)

    def back_copy(p, d):
        dst = back_in.at[pl.ds(pl.multiple_of(core * half_v + p * PART, 16), PART), :]
        return remote(back.at[prds(p), cols(d)], dst, back_sem.at[p, d], prev_dev[d], back_sem.at[p, core])

    def back_arrival(p, s):
        dst = back_in.at[pl.ds(pl.multiple_of(s * half_v + p * PART, 16), PART), :]
        return remote(back.at[prds(p), cols(s)], dst, back_sem.at[p, s], prev_dev[s])

    def acc_copy(b):
        return remote(acc.at[b, :, cols(1 - core)], acc_in.at[b], acc_sem.at[b], sibling)

    barrier = pltpu.get_barrier_semaphore()
    others = (sibling, partner) + x_dev + next_dev + prev_dev
    for device in others:
        pl.semaphore_signal(barrier, inc=1, device_id=device, device_id_type=MESH)
    local = pltpu.make_async_copy(own, left.at[:, cols(core)], local_sem)
    local.start()

    for i in range(half_v // min(128, half_v)):
        m = min(128, half_v)
        line = eps_vir[:, pl.ds(pl.multiple_of(core * half_v + i * m, m), m)]
        eps_rows[pl.ds(i * m, m), :] = jnp.broadcast_to(line, (m, m)).T
    for b in range(BLOCKS):
        acc[b] = jnp.zeros((width, NC * k), jnp.float32)
    slot = start[0]
    occ_sum = eps_occ[slot + assignment[o]] + eps_occ[slot + assignment[o_prev]]
    eps_cols = eps_vir[:, pl.ds(pl.multiple_of(mine * width, width), width)] - occ_sum

    pl.semaphore_wait(barrier, len(others))

    def send_right(p):
        for d in range(NC):
            right_copy(p, d).start()

    left_copy().start()
    for p in range(min(AHEAD, parts)):
        send_right(p)
    local.wait()
    left_copy().wait_recv()

    def tile_block(p, x_):
        block = left[pl.ds(pl.multiple_of(x_ * NY * width, NY * width), NY * width), :]
        return dot(right[prds(p), :], block, ((1,), (1,)))

    def stage_tile(c):
        p = c // per_part

        @pl.when(lax.rem(c, per_part) == 0)
        def _():
            @pl.when(p + AHEAD < parts)
            def _():
                send_right(p + AHEAD)

            for s in range(NC):
                right_arrival(p, s).wait_recv()

            @pl.when(p >= first_last // PART)
            def _():
                right_last_copy(p).start()

            values = tile_block(p, x_far).astype(jnp.bfloat16)
            for j in range(NY):
                far_out[j, prds(p), :] = values[:, j * width : (j + 1) * width]

        for d in range(2):
            far_copy(c, d).start()

        @pl.when(lax.rem(c, per_part) == 0)
        def _():
            for x_ in (x_next, x_prev, x):
                values = tile_block(p, x_)
                for j in range(NY):
                    tile[x_ * NY + j, prds(p), :] = values[:, j * width : (j + 1) * width]

    def stage_near(c):
        for d in range(2):
            far_copy(c, d).wait_recv()
            x_ = (x_next, x_prev)[d]
            r = rds(c, half, d * half)
            for j in range(NY):
                tile[x_ * NY + j, r, :] += far[j, r, :].astype(jnp.float32)
            codes, unit = fixed([tile[x_ * NY + j, rds(c), :] for j in range(NY)])
            for j in range(NY):
                near_out[d, j, rds(c), :] = codes[j]
            near_unit_out[c, d] = jnp.broadcast_to(unit, near_unit_out.shape[2:])
            near_unit_copy(c, d).start()
            near_copy(c, d).start()

    def near_sum(c, y_):
        r = rds(c)
        total = tile[x * NY + y_, r, :]
        for d in range(2):
            total += near[d, y_, r, :].astype(jnp.float32) * near_unit[c, d][0:1, 0:1]
        return total

    def stage_sum(c):
        for d in range(2):
            near_unit_copy(c, d).wait_recv()
            near_copy(c, d).wait_recv()
        (codes,), unit = fixed([near_sum(c, 1 - y)])
        tail_out[rds(c), :] = codes
        tail_unit_out[c] = jnp.broadcast_to(unit, tail_unit_out.shape[1:])
        tail_unit_copy(c).start()
        tail_copy(c).start()
        tile[mine, rds(c), :] = near_sum(c, y)

    def stage_amp(c):
        tail_unit_copy(c).wait_recv()
        tail_copy(c).wait_recv()
        r = rds(c)
        total = tile[mine, r, :] + tail[r, :].astype(jnp.float32) * tail_unit[c][0:1, 0:1]
        denominator = eps_rows[r, 0:1] + eps_cols
        amp[mine, r, :] = (total / denominator).astype(jnp.bfloat16)
        amp_y_copy(c).start()

    def stage_spread(c):
        amp_y_copy(c, theirs).wait_recv()
        for d in range(2):
            amp_x_copy(c, d).start()

    def stage_forward(c):
        for d in range(2):
            amp_x_copy(c, d, (x_prev, x_next)[d]).wait_recv()
            amp_f_copy(c, d, (x_prev, x_next)[d]).start()

    def own_block(first, b):
        r = pl.ds(pl.multiple_of(first * rows, 16), GROUP)
        acc[b] += dot(amp[b, r, :], right[r, :], ((0,), (0,)))

    def stage_gamma(c):
        for d in range(2):
            amp_f_copy(c, d, x_far).wait_recv()

        @pl.when(c >= n - per_group)
        def _():
            amp_last_copy(c).start()

        @pl.when(lax.rem(c + 1, per_part) == 0)
        def _():
            p = c // per_part
            r = prds(p)
            total = dot(amp[0, r, :], left[pl.ds(0, width), :], ((1,), (0,)))
            for b in range(1, BLOCKS):
                total += dot(amp[b, r, :], left[pl.ds(b * width, width), :], ((1,), (0,)))
            back[r, :] = total.astype(jnp.bfloat16)
            for d in range(NC):
                back_copy(p, d).start()

        @pl.when((lax.rem(c + 1, per_group) == 0) & (c + 1 < n))
        def _():
            for b in range(BLOCKS):
                own_block(c + 1 - per_group, b)

            @pl.when(c + 1 == n - per_group)
            def _():
                for b in range(BLOCKS):
                    acc_copy(b).start()

    stages = (stage_tile, stage_gamma, stage_forward, stage_spread, stage_amp, stage_sum, stage_near)
    offsets = (0, 14, 11, 8, 6, 4, 2)

    def tick(t, carry):
        for stage, offset in zip(stages, offsets):
            c = t - offset

            @pl.when((c >= 0) & (c < n))
            def _():
                stage(c)

        return carry

    lax.fori_loop(0, n + max(offsets), tick, 0)

    for p in range(first_last // PART, parts):
        right_last_copy(p).wait_recv()
    for c in range(n - per_group, n):
        amp_last_copy(c).wait_recv()
    for b in range(BLOCKS):
        acc_copy(b).wait_recv()

    last = pl.ds(first_last, GROUP)
    for b in range(BLOCKS):
        total = acc[b, :, cols(core)] + acc_in[b]
        total += dot(amp[b, last, :], right[last, cols(core)], ((0,), (0,)))
        total += dot(amp_last[b], right_last[...], ((0,), (0,)))
        out[pl.ds(b * width, width), :] = total

    def arrived(p, carry):
        for s in range(NC):
            back_arrival(p, s).wait_recv()
        return carry

    lax.fori_loop(0, parts, arrived, 0)
    for b in range(BLOCKS):
        r = pl.ds(b * width, width)
        out[r, :] += back_in[r, :].astype(jnp.float32)

    left_copy().wait_send()
    for b in range(BLOCKS):
        acc_copy(b).wait_send()
    for p in range(first_last // PART, parts):
        right_last_copy(p).wait_send()
    for c in range(n - per_group, n):
        amp_last_copy(c).wait_send()

    def part_sent(p, carry):
        for d in range(NC):
            right_copy(p, d).wait_send()
            back_copy(p, d).wait_send()
        return carry

    lax.fori_loop(0, parts, part_sent, 0)

    def sent(c, carry):
        for d in range(2):
            far_copy(c, d).wait_send()
            near_copy(c, d).wait_send()
            near_unit_copy(c, d).wait_send()
            amp_x_copy(c, d).wait_send()
            amp_f_copy(c, d, (x_prev, x_next)[d]).wait_send()
        tail_copy(c).wait_send()
        tail_unit_copy(c).wait_send()
        amp_y_copy(c).wait_send()
        return carry

    lax.fori_loop(0, n, sent, 0)


def per_device(n_occ, rows, factors, eps_occ, eps_vir, window_start, assignment):
    own = factors[0]
    v, k = own.shape
    half_v, width = v // NC, v // BLOCKS
    n = half_v // rows
    f32, bf16 = jnp.float32, jnp.bfloat16
    dma = pltpu.SemaphoreType.DMA
    smem = pl.BlockSpec(memory_space=pltpu.SMEM)
    out = pl.pallas_call(
        functools.partial(kernel, n_occ, rows),
        out_shape=jax.ShapeDtypeStruct((v, k), f32),
        in_specs=[smem, smem, smem, pl.BlockSpec(memory_space=pl.ANY), pl.BlockSpec(memory_space=pltpu.VMEM)],
        out_specs=pl.BlockSpec(memory_space=pltpu.VMEM),
        scratch_shapes=[
            pltpu.VMEM((v, NC * k), bf16),
            pltpu.VMEM((half_v, NC * k), bf16),
            pltpu.VMEM((BLOCKS, half_v, width), f32),
            pltpu.VMEM((NY, half_v, width), bf16),
            pltpu.VMEM((NY, half_v, width), bf16),
            pltpu.VMEM((2, NY, half_v, width), jnp.int16),
            pltpu.VMEM((2, NY, half_v, width), jnp.int16),
            pltpu.VMEM((n, 2, 8, 128), f32),
            pltpu.VMEM((n, 2, 8, 128), f32),
            pltpu.VMEM((half_v, width), jnp.int16),
            pltpu.VMEM((half_v, width), jnp.int16),
            pltpu.VMEM((n, 8, 128), f32),
            pltpu.VMEM((n, 8, 128), f32),
            pltpu.VMEM((BLOCKS, half_v, width), bf16),
            pltpu.VMEM((BLOCKS, width, NC * k), f32),
            pltpu.VMEM((half_v, NC * k), bf16),
            pltpu.VMEM((v, k), bf16),
            pltpu.VMEM((BLOCKS, width, k), f32),
            pltpu.VMEM((half_v, min(128, half_v)), f32),
            pltpu.VMEM((GROUP, k), bf16),
            pltpu.VMEM((BLOCKS, GROUP, width), bf16),
            dma(()),
            dma((2,)),
            dma((half_v // PART, 2, 2)),
            dma((n, 2, 2)),
            dma((n, 2, 2)),
            dma((n, 2, 2)),
            dma((n, 2)),
            dma((n, 2)),
            dma((n, 2)),
            dma((n, 2, 2)),
            dma((n, 2, 2)),
            dma((half_v // PART, 2, 2)),
            dma((BLOCKS, 2)),
            dma((GROUP // PART, 2)),
            dma((GROUP // rows, 2)),
        ],
        compiler_params=pltpu.CompilerParams(
            collective_id=0, has_side_effects=True, vmem_limit_bytes=60 * 2**20
        ),
        cost_estimate=pl.CostEstimate(
            flops=3 * 2 * v * v * k, bytes_accessed=6 * v * k, transcendentals=0
        ),
    )(eps_occ, window_start, assignment, own, eps_vir[None, :])
    return out[None]


def solution(mesh):
    in_specs = (P("occ", None, "aux"), P(), P(), P(), P())
    out_specs = P("occ", None, "aux")
    return jax.shard_map(
        functools.partial(per_device, mesh.shape["occ"], ROWS),
        mesh=mesh, in_specs=in_specs, out_specs=out_specs, check_vma=False,
    )
```
